128 devices in a mesh: buf: 8 (over z, core), lat: 4 (over y), lon: 4 (over x).
Axes of the slice: x: 4, y: 4, z: 4, core: 2. Of those that a mesh axis runs over, the one named last changes fastest.
Arguments:
- slots: bfloat16 [8, 4, 4, 2, 1024, 512], P('buf', 'lat', 'lon'), may hold values from -40 to 40
- plan_rank: int32 [4, 4, 8, 1], P('lat', 'lon'), may hold values from 0 to 7; in each aligned block of 8 rows (0 to 7, 8 to 15, ..., all dimensions but the last counted through in order) at most 4 rows name the same one
- plan_slot: int32 [4, 4, 8], P('lat', 'lon'), may hold values from 0 to 1
- gain: float32 [512], replicated, may hold values from 0.5 to 2
- w_qkv: float32 [512, 1536], replicated, may hold values from -0.25 to 0.25
- w_proj: float32 [512, 512], replicated, may hold values from -0.25 to 0.25
- rel_bias: float32 [16, 64, 64], replicated, may hold values from -320 to 320
- cotangent: float32 [8, 1, 128, 128, 512], P('buf', None, 'lat', 'lon'), may hold values from -6 to 6
Outputs:
- block_out: float32 [8, 1, 128, 128, 512], P('buf', None, 'lat', 'lon')
- grad_qkv: float32 [512, 1536], P(('buf', 'lat', 'lon'))
- grad_proj: float32 [512, 512], P(('buf', 'lat', 'lon'))
- grad_gain: float32 [512], P(('buf', 'lat', 'lon'))
- grad_rel: float32 [1024, 64], P(('buf', 'lat', 'lon'))
The draws below stay inside these ranges and needn't reach their ends.
Inputs may be any that keep to these rules, and one draw needn't show every extreme that they name: `plan_rank`: among the 8 samples of one tile, no buffer owner is named more than 4 times; in every draw some tile has exactly 4 samples reading one owner.
All inputs are finite; a program needn't handle non-finite values.
Results may differ from the reference program's by a relative error of at most 0.0011.
Values may be sent and summed in bfloat16 or wider, within the bound.
No kernel may reach another device: no remote copies, remote signals or barrier semaphores. Data moves between devices by JAX's collectives and lax.ppermute only.
A program may use at most 128 MiB of HBM per device.

```python
import math
import jax
import jax.numpy as jnp
import numpy as np
from jax import lax

C = 512
HEADS = 16
WSIDE = 8
WAREA = 64
LEV = 1
TH = 32
TW = 32
SLOTS = 2
TILE_TOK = 1024
CAP = 4
NH = 128
NW = 128
ALL_TOK = 131072
N_BUF = 8
N_LAT = 4
N_LON = 4


def draw_slots(key, part):
    key = jax.random.fold_in(key, 11)
    row_key, chan_key, value_key = jax.random.split(key, 3)
    full_shape = (N_BUF, N_LAT, N_LON, SLOTS, TILE_TOK, C)
    row_scale = jnp.exp(jax.random.uniform(row_key, full_shape[:-1] + (1,), jnp.float32, math.log(0.3), math.log(3.0)))
    chan_scale = jnp.exp(jax.random.uniform(chan_key, (C,), jnp.float32, math.log(0.3), math.log(3.0)))
    values = jax.random.truncated_normal(value_key, -4.0, 4.0, full_shape, jnp.float32)
    return (values * row_scale * chan_scale).astype(jnp.bfloat16)


def draw_rel_bias(key, part):
    key = jax.random.fold_in(key, 23)
    base_key = jax.random.fold_in(key, 0)
    full_shape = (HEADS, WAREA, WAREA)
    return jax.random.truncated_normal(base_key, -4.0, 4.0, full_shape, jnp.float32)


def touch_ends(values, own_key, smallest, largest):
    shape = values.shape
    place = [jax.random.randint(jax.random.fold_in(own_key, axis), (), 0, shape[axis]) for axis in range(len(shape))]
    values = values.at[tuple(place)].set(smallest)
    longest = shape.index(max(shape))
    place[longest] = (place[longest] + 1) % shape[longest]
    return values.at[tuple(place)].set(largest)


def block_levels(own_key, shape, shards, smallest, top_value):
    factor_of = 1.0
    for axis_at, shards_of in shards:
        heights = jax.random.uniform(jax.random.fold_in(jax.random.fold_in(own_key, 6), axis_at), (shards_of,), jnp.float32, smallest / len(shards), top_value / len(shards))
        factor_of = factor_of * jnp.repeat(jnp.exp(heights), shape[axis_at] // shards_of).reshape((-1,) + (1,) * (len(shape) - 1 - axis_at))
    return factor_of


def routed_block(stream_key, own, number, rows, count, top, reach, lean):
    sequence = jax.random.permutation(stream_key, count)
    heavy_load, usual = shares(count, rows * top, reach, lean, True), shares(count, rows * top, reach, lean, False)
    places = jnp.arange(count)

    def named(tallies, offset_by):
        used = int((tallies > 0).sum())
        fixed = max(1, used // 4)
        moved = fixed + (places - fixed + offset_by * (used - fixed)) % max(1, count - fixed)
        return jnp.zeros((count,), jnp.int32).at[sequence[jnp.where(places < fixed, places, moved)]].set(jnp.asarray(tallies, jnp.int32))

    tallies = jnp.where(number % 4 == 0, named(heavy_load, number // 4), named(usual, number - number // 4 - 1))
    mixed = jax.random.permutation(jax.random.fold_in(own, 3), count)
    source_of, receiver = mixed[0:count // 2 * 2:2], mixed[1:count // 2 * 2:2]
    room = jnp.minimum(tallies[source_of] - 1, reach - tallies[receiver]) // 2
    room = jnp.where((source_of == sequence[0]) | (receiver == sequence[0]) | (tallies[receiver] == 0), 0, jnp.maximum(room, 0))
    moved = jax.random.randint(jax.random.fold_in(own, 4), (count // 2,), 0, 1 << 20) % (room + 1)
    tallies = tallies.at[source_of].add(-moved).at[receiver].add(moved)
    labels = jnp.searchsorted(jnp.cumsum(tallies), jnp.arange(rows * top), side="right").astype(jnp.int32)
    listing = labels.reshape(top, rows).T
    listing = listing[jax.random.permutation(jax.random.fold_in(own, 1), rows)]
    offset_by = jax.random.randint(jax.random.fold_in(own, 2), (rows, 1), 0, top)
    return jnp.take_along_axis(listing, (jnp.arange(top)[None, :] + offset_by) % top, axis=1)


def shares(amount, total, most, lean, full):
    weights = [(1 << 20) // math.isqrt(grade ** lean) + 1 for grade in range(1, amount + 1)]
    largest = most if full else min(most, max(-(-total // amount), total * weights[0] // sum(weights)))
    least = 1 if total - largest >= amount - 1 else 0
    given, rest = [largest] + [least] * (amount - 1), total - largest - least * (amount - 1)
    while rest > 0:
        movable = [i for i in range(1, amount) if given[i] < largest] or [i for i in range(1, amount) if given[i] < most]
        whole, left = sum([weights[i] for i in movable]), rest
        for i in movable:
            extra = min(most - given[i], max(1, left * weights[i] // whole), rest)
            given[i] = given[i] + extra
            rest = rest - extra
    return np.array(given)


def scatter_about(stream_key, extent, scale, reach, shards=(), kind=jnp.bfloat16):
    values = jax.random.normal(stream_key, extent, jnp.float32) * scale
    if len(shards) > 0:
        values = block_levels(stream_key, extent, shards, -0.22, 0.18) * values
    return jnp.clip(values, min=-reach, max=reach).astype(kind)


def setup_inputs(seed: int = 0) -> dict:
    splits = jax.random.split(jax.random.key(seed), 9)
    slots = draw_slots(jax.random.fold_in(splits[8], 71), 0)
    plan_rank_keys = jax.random.split(jax.random.fold_in(splits[1], 1), N_LAT * N_LON * N_BUF // N_BUF)
    plan_rank_turns = jax.random.permutation(jax.random.fold_in(splits[1], 3), N_LAT * N_LON * N_BUF // N_BUF)
    plan_rank = jax.vmap(lambda own, number: routed_block(jax.random.fold_in(splits[1], 2), own, number, N_BUF, N_BUF, 1, CAP, 2))(plan_rank_keys, plan_rank_turns).reshape((N_LAT, N_LON, N_BUF, 1))
    plan_slot = touch_ends(jax.random.randint(splits[2], (N_LAT, N_LON, N_BUF), 0, SLOTS), jax.random.fold_in(splits[2], 1), 0, SLOTS - 1).astype(jnp.int32)
    gain = jnp.clip(jnp.exp(jax.random.uniform(splits[3], (C,), jnp.float32, math.log(0.5), math.log(2.0))), 0.5, 2.0)
    w_qkv = scatter_about(splits[4], (C, 3 * C), C ** -0.5, 0.25, (), jnp.float32)
    w_proj = scatter_about(splits[5], (C, C), C ** -0.5, 0.25, (), jnp.float32)
    rel_bias = draw_rel_bias(jax.random.fold_in(splits[8], 71), 0)
    cotangent = scatter_about(splits[7], (N_BUF, LEV, NH, NW, C), 1.0, 6.0, ((0, 8), (2, 4), (3, 4)), jnp.float32)
    return dict(slots=slots, plan_rank=plan_rank, plan_slot=plan_slot, gain=gain, w_qkv=w_qkv, w_proj=w_proj, rel_bias=rel_bias, cotangent=cotangent)


precise = lax.Precision.HIGHEST

def window_view(field, window_side):
    levels, row_count, col_count, width = field.shape
    tiled = field.reshape(levels, row_count // window_side, window_side, col_count // window_side, window_side, width)
    tiled = tiled.transpose(0, 1, 3, 2, 4, 5)
    return tiled.reshape(levels * (row_count // window_side) * (col_count // window_side), window_side * window_side, width)

def grid_view(windows, levels, row_count, col_count, window_side):
    width = windows.shape[-1]
    tiled = windows.reshape(levels, row_count // window_side, col_count // window_side, window_side, window_side, width)
    return tiled.transpose(0, 1, 3, 2, 4, 5).reshape(levels, row_count, col_count, width)

def window_mask(flagged, window_side):
    positions = jnp.arange(window_side * window_side) // window_side
    region = positions >= window_side // 2
    crossing = region[:, None] != region[None, :]
    return flagged[:, None, None] & crossing[None]

def normalize(tokens, gain):
    centered = tokens - lax.optimization_barrier(jnp.mean(tokens, axis=-1, keepdims=True))
    spread = lax.optimization_barrier(jnp.mean(centered * centered, axis=-1, keepdims=True))
    unit_rows = centered * lax.rsqrt(spread + 1e-05)
    return (unit_rows, unit_rows * gain)

def attend_core(packed, rel_bias, masked, head_count):
    window_count, window_area, packed_width = packed.shape
    width = packed_width // 3
    head_size = width // head_count
    queries = packed[..., :width].reshape(window_count, window_area, head_count, head_size)
    key_part = packed[..., width:2 * width].reshape(window_count, window_area, head_count, head_size)
    values = packed[..., 2 * width:].reshape(window_count, window_area, head_count, head_size)
    scores = jnp.einsum('nphd,nqhd->nhpq', queries, key_part, precision=precise) / math.sqrt(head_size)
    scores = scores + rel_bias[None]
    scores = jnp.where(masked[:, None], -1000000000.0, scores)
    row_max = lax.optimization_barrier(jnp.max(scores, axis=-1, keepdims=True))
    exponent = jnp.exp(scores - row_max)
    weights = exponent / lax.optimization_barrier(jnp.sum(exponent, axis=-1, keepdims=True))
    mixed_heads = jnp.einsum('nhpq,nqhd->nphd', weights, values, precision=precise)
    return mixed_heads.reshape(window_count, window_area, width)

def block(state, gain, w_qkv, w_proj, rel_bias):
    half_side = WSIDE // 2
    shifted = jnp.roll(state, (-half_side, -half_side), axis=(1, 2))
    levels, row_count, col_count, width = shifted.shape
    windowed = window_view(shifted, WSIDE)
    unit_rows, normed = normalize(windowed, gain)
    packed = jnp.dot(normed, w_qkv, precision=precise)
    window_count = windowed.shape[0]
    window_rows = jnp.arange(window_count) // (col_count // WSIDE) % (row_count // WSIDE)
    masked = window_mask(window_rows == row_count // WSIDE - 1, WSIDE)
    attended = attend_core(packed, rel_bias, masked, HEADS)
    result = windowed + jnp.dot(attended, w_proj, precision=precise)
    return grid_view(result, levels, row_count, col_count, WSIDE)

def reference(slots, plan_rank, plan_slot, gain, w_qkv, w_proj, rel_bias, cotangent):
    cot_scale = 1.0 / math.sqrt(ALL_TOK)
    lat_index = jnp.arange(N_LAT, dtype=jnp.int32)[:, None]
    lon_index = jnp.arange(N_LON, dtype=jnp.int32)[None, :]
    sample_ranks_all = jnp.moveaxis(plan_rank[..., 0], 2, 0)
    sample_slots_all = jnp.moveaxis(plan_slot, 2, 0)

    def one_sample(inputs):
        sample_ranks, sample_slots, sample_cot = inputs
        chosen = slots[sample_ranks, lat_index, lon_index, sample_slots]
        pieces = chosen.astype(jnp.float32).reshape(N_LAT, N_LON, LEV, TH, TW, C)
        state = pieces.transpose(2, 0, 3, 1, 4, 5).reshape(LEV, NH, NW, C)

        def forward(gain_in, qkv_in, proj_in, bias_in):
            return block(state, gain_in, qkv_in, proj_in, bias_in)
        output, pullback = jax.vjp(forward, gain, w_qkv, w_proj, rel_bias)
        grads = pullback(sample_cot * cot_scale)
        return (output, grads)
    outputs, grads = lax.map(one_sample, (sample_ranks_all, sample_slots_all, cotangent))
    grad_gain = lax.optimization_barrier(jnp.sum(grads[0], axis=0))
    grad_qkv = lax.optimization_barrier(jnp.sum(grads[1], axis=0))
    grad_proj = lax.optimization_barrier(jnp.sum(grads[2], axis=0))
    grad_rel = lax.optimization_barrier(jnp.sum(grads[3], axis=0)).reshape(HEADS * WAREA, WAREA)
    return (outputs, grad_qkv, grad_proj, grad_gain, grad_rel)
```

```python
import functools
import math

import jax
import jax.numpy as jnp
from jax import lax
from jax.experimental import pallas as pl
from jax.experimental.pallas import tpu as pltpu
from jax.sharding import PartitionSpec as P

HEADS = 16
WSIDE = 8
NT = (((1,), (1,)), ((), ()))
NN = (((1,), (0,)), ((), ()))
f32, bf16 = jnp.float32, jnp.bfloat16


def dot(left, right, dims=NN):
    return lax.dot_general(left, right, dims, preferred_element_type=f32)


def halves(value):
    high = value.astype(bf16)
    return high, (value - high.astype(f32)).astype(bf16)


def window_rows(block):
    pieces = [block[u, 8 * w : 8 * w + 8, :] for w in range(4) for u in range(8)]
    return jnp.concatenate(pieces, axis=0)


def upstream_kernel(scale, cot_ref, wp3_ref, uhi_ref, ulo_ref, dohi_ref, dolo_ref):
    upstream = window_rows(cot_ref) * scale
    uhi, ulo = halves(upstream)
    uhi_ref[...] = uhi
    ulo_ref[...] = ulo
    u3 = jnp.concatenate([uhi, uhi, ulo], axis=1)
    for at in range(0, 512, 128):
        dohi_ref[at : at + 128, :], dolo_ref[at : at + 128, :] = halves(
            dot(wp3_ref[at : at + 128, :], u3, NT)
        )


def swap(value):
    return jnp.concatenate([value[:, 64:], value[:, :64]], axis=1)


def block_diagonal(value, left, right):
    other = swap(value)
    zeros = jnp.zeros((32, 128), bf16)
    for even, odd in ((value, other), (other, value)):
        first = jnp.concatenate([even[0:32] * left, odd[32:64] * right, zeros, zeros], axis=0)
        second = jnp.concatenate([zeros, zeros, even[64:96] * left, odd[96:128] * right], axis=0)
        yield jnp.concatenate([first, second], axis=1)


def gather_diagonal(lane, pair_a, pair_b):
    low = lane < 64
    return jnp.concatenate(
        [
            jnp.where(low, pair_a[:32], swap(pair_b[:32])),
            jnp.where(low, swap(pair_a[32:]), pair_b[32:]),
        ],
        axis=0,
    )


def heads_product(left2, hi, lo, window):
    zeros = jnp.zeros((64, 128), bf16)
    for t in range(2):
        h, l = hi[:, 128 * t : 128 * t + 128], lo[:, 128 * t : 128 * t + 128]
        right = jnp.concatenate([h, l, h, zeros] if window == 0 else [h, l, zeros, h], axis=0)
        yield dot(left2[64 * t : 64 * t + 64], right)


def main_kernel(
    flag_ref, x_ref, wcat_ref, wp3_ref, bias_ref, uhi_ref, ulo_ref, dohi_ref, dolo_ref,
    out_ref, g_ref,
    pkhi, pklo, kt, vt, rstd_tok, rstd_lane, xt_all, ahi_all, alo_all, gq_all, gkv_all, rel_acc,
):
    step = pl.program_id(0)
    here = pl.ds(pl.multiple_of(step * 256, 256), 256)
    here_lo = pl.ds(pl.multiple_of(step * 256 + 1024, 256), 256)

    @pl.when(step == 0)
    def _():
        rel_acc[...] = jnp.zeros_like(rel_acc)

    tokens = window_rows(x_ref[...].astype(f32))
    tokens16 = tokens.astype(bf16)
    eye = (
        lax.broadcasted_iota(jnp.int32, (256, 256), 0) == lax.broadcasted_iota(jnp.int32, (256, 256), 1)
    ).astype(f32).astype(bf16)
    xt = jnp.concatenate([dot(eye, tokens16[:, :256], NT), dot(eye, tokens16[:, 256:], NT)], axis=0)
    xt16 = xt.astype(bf16)
    xt_all[:, here] = xt16
    mean = jnp.sum(xt, axis=0, keepdims=True) * (1.0 / 512)
    centered = xt - mean
    spread = jnp.sum(centered * centered, axis=0, keepdims=True) * (1.0 / 512)
    rstd = lax.rsqrt(spread + 1e-05)
    rstd_lane[...] = rstd * jnp.ones((8, 1), f32)
    rstd_tok[...] = jnp.transpose(jnp.broadcast_to(rstd, (128, 256)))
    twice = jnp.concatenate([xt16, xt16], axis=0)
    for at in range(0, 1536, 128):
        rows = slice(at, at + 128)
        pkhi[rows, :], pklo[rows, :] = halves(dot(wcat_ref[rows, :], twice) * rstd)
    for base, tok in ((512, kt), (1024, vt)):
        for g in range(4):
            rows = slice(base + 128 * g, base + 128 * g + 128)
            high = dot(eye, pkhi[rows, :], NT).astype(bf16)
            low = dot(eye, pklo[rows, :], NT).astype(bf16)
            tok[g, :, 0:128] = high
            tok[g, :, 128:256] = low
            tok[g, :, 256:384] = high

    lane = lax.broadcasted_iota(jnp.int32, (1, 128), 1)
    left16 = (lane < 64).astype(f32).astype(bf16)
    right16 = (lane >= 64).astype(f32).astype(bf16)
    edge = (flag_ref[0] > 0) & (step == 3)
    row_of = lax.broadcasted_iota(jnp.int32, (64, 256), 0)
    lane_of = lax.broadcasted_iota(jnp.int32, (64, 256), 1)
    crossing = ((row_of >= 32) != ((lane_of & 63) >= 32)) & edge
    root = 1.0 / math.sqrt(32.0)

    def group(g, carry):
        rows_q = pl.ds(pl.multiple_of(g * 128, 128), 128)
        rows_k = pl.ds(pl.multiple_of(g * 128 + 512, 128), 128)
        rows_v = pl.ds(pl.multiple_of(g * 128 + 1024, 128), 128)
        cols_k = rows_q
        cols_v = pl.ds(pl.multiple_of(g * 128 + 512, 128), 128)
        rel = jnp.zeros((64, 256), f32)
        for p in range(2):
            lanes = slice(128 * p, 128 * p + 128)
            qhi = list(block_diagonal(pkhi[rows_q, lanes], left16, right16))
            qlo = list(block_diagonal(pklo[rows_q, lanes], left16, right16))
            ohi = list(block_diagonal(dohi_ref[rows_q, lanes], left16, right16))
            olo = list(block_diagonal(dolo_ref[rows_q, lanes], left16, right16))
            both = {}
            for name, rows in (("k", rows_k), ("v", rows_v)):
                high, low = pkhi[rows, lanes], pklo[rows, lanes]
                other = swap(high)
                first = high * left16 + other * right16
                second = other * left16 + high * right16
                both[name] = [jnp.concatenate([first, low], axis=1), jnp.concatenate([second, low], axis=1)]
            attended, grad_q = [], []
            for w in range(2):
                at = 128 * p + 64 * w
                s = dot(kt[g, at : at + 64, :], jnp.concatenate([qhi[w], qhi[w], qlo[w]], axis=0))
                s = jnp.where(crossing, -1000000000.0, s + bias_ref[g])
                e = jnp.exp(s - jnp.max(s, axis=0, keepdims=True))
                weights = e * (1.0 / jnp.sum(e, axis=0, keepdims=True))
                phi, plo = halves(weights)
                attended.append(list(heads_product(both["v"][w], phi, plo, w)))
                dp = dot(vt[g, at : at + 64, :], jnp.concatenate([ohi[w], ohi[w], olo[w]], axis=0))
                inner = jnp.sum(weights * dp, axis=0, keepdims=True)
                ds = weights * (dp - inner)
                rel = rel + ds
                shi, slo = halves(ds)
                grad_q.append(list(heads_product(both["k"][w], shi, slo, w)))
                scale = rstd_tok[at : at + 64, :]
                to = pl.ds(pl.multiple_of(step * 256 + at, 64), 64)
                to_lo = pl.ds(pl.multiple_of(step * 256 + at + 1024, 64), 64)
                for hi, lo, chi, clo, cols in (
                    (phi, plo, ohi[w], olo[w], cols_v),
                    (shi, slo, qhi[w], qlo[w], cols_k),
                ):
                    full = dot(
                        jnp.concatenate([hi, lo], axis=0), jnp.concatenate([chi, clo], axis=0), NT
                    )
                    total = full[:64, :128] + full[64:, :128] + full[:64, 128:]
                    gkv_all[to, cols], gkv_all[to_lo, cols] = halves(total * scale)
            here_p = pl.ds(pl.multiple_of(step * 256 + 128 * p, 128), 128)
            here_p_lo = pl.ds(pl.multiple_of(step * 256 + 128 * p + 1024, 128), 128)
            att = jnp.concatenate([gather_diagonal(lane, attended[0][t], attended[1][t]) for t in range(2)], axis=0)
            ahi_all[rows_q, here_p], alo_all[rows_q, here_p] = halves(att)
            gq = jnp.concatenate([gather_diagonal(lane, grad_q[0][t], grad_q[1][t]) for t in range(2)], axis=0)
            gq = gq * (rstd_lane[0:1, lanes] * root)
            gq_all[rows_q, here_p], gq_all[rows_q, here_p_lo] = halves(gq)
        rel_acc[g] = rel_acc[g] + rel
        return carry

    lax.fori_loop(0, 4, group, 0)

    tok_hi = dot(eye, ahi_all[:, here], NT).astype(bf16)
    tok_lo = dot(eye, alo_all[:, here], NT).astype(bf16)
    result = tokens + dot(
        jnp.concatenate([tok_hi, tok_lo, tok_hi], axis=1), wp3_ref[...]
    )
    for w in range(4):
        for u in range(8):
            out_ref[u, 8 * w : 8 * w + 8, :] = result[64 * w + 8 * u : 64 * w + 8 * u + 8, :]

    @pl.when(step == 3)
    def _():
        sub = lax.broadcasted_iota(jnp.int32, (1, 8, 128), 1)

        def pack(k, value):
            a, b = value[:, :128].reshape(64, 8, 128), value[:, 128:].reshape(64, 8, 128)
            aa = jnp.concatenate([a[:, 4:], a[:, :4]], axis=1)
            bb = jnp.concatenate([b[:, 4:], b[:, :4]], axis=1)
            even = jnp.where(sub < 4, a, bb).reshape(4, 2, 8, 8, 128)
            odd = jnp.where(sub < 4, aa, b).reshape(4, 2, 8, 8, 128)
            for c in range(2):
                g_ref[c, :, :, 0, 8 * k : 8 * k + 8, :] = even[:, c]
                g_ref[c, :, :, 1, 8 * k : 8 * k + 8, :] = odd[:, c]

        twice = jnp.concatenate([xt_all[...], xt_all[...]], axis=1)
        for k in range(6):
            if k < 2:
                value = dot(twice, gq_all[256 * k : 256 * k + 256, :], NT)
            else:
                value = dot(twice, gkv_all[:, 256 * k - 512 : 256 * k - 256])
            pack(k, value - jnp.sum(value, axis=0, keepdims=True) * (1.0 / 512))
        for k in range(2):
            cols = slice(256 * k, 256 * k + 256)
            u = uhi_ref[:, cols]
            value = (
                dot(ahi_all[...], u) + dot(alo_all[...], u) + dot(ahi_all[...], ulo_ref[:, cols])
            )
            pack(6 + k, value)
        for g in range(4):
            turned = jnp.transpose(
                jnp.concatenate([rel_acc[g], jnp.zeros((64, 256), f32)], axis=0)
            ).reshape(2, 8, 2, 8, 128)
            for c in range(2):
                g_ref[c, g, :, :, 64:72, :] = turned[c]


def full(shape):
    return pl.BlockSpec(shape, lambda a: (0,) * len(shape))


def upstream_call(cot, wp3, scale):
    return pl.pallas_call(
        functools.partial(upstream_kernel, scale),
        grid=(4,),
        in_specs=[pl.BlockSpec((8, 32, 512), lambda a: (a, 0, 0)), full((512, 1536))],
        out_specs=[
            pl.BlockSpec((256, 512), lambda a: (a, 0)),
            pl.BlockSpec((256, 512), lambda a: (a, 0)),
            pl.BlockSpec((512, 256), lambda a: (0, a)),
            pl.BlockSpec((512, 256), lambda a: (0, a)),
        ],
        out_shape=[jax.ShapeDtypeStruct((1024, 512), bf16)] * 2
        + [jax.ShapeDtypeStruct((512, 1024), bf16)] * 2,
        compiler_params=pltpu.CompilerParams(vmem_limit_bytes=40 << 20),
        cost_estimate=pl.CostEstimate(flops=1600000000, bytes_accessed=8 << 20, transcendentals=0),
        name="upstream",
    )(cot, wp3)


def main_call(flag, x, wcat, wp3, bias, uhi, ulo, dohi, dolo):
    return pl.pallas_call(
        main_kernel,
        grid=(4,),
        in_specs=[
            pl.BlockSpec(memory_space=pltpu.SMEM),
            pl.BlockSpec((8, 32, 512), lambda a: (a, 0, 0)),
            full((1536, 1024)),
            full((1536, 512)),
            full((4, 64, 256)),
            full((1024, 512)),
            full((1024, 512)),
            pl.BlockSpec((512, 256), lambda a: (0, a)),
            pl.BlockSpec((512, 256), lambda a: (0, a)),
        ],
        out_specs=[
            pl.BlockSpec((8, 32, 512), lambda a: (a, 0, 0)),
            full((2, 4, 8, 2, 72, 128)),
        ],
        out_shape=[
            jax.ShapeDtypeStruct((32, 32, 512), f32),
            jax.ShapeDtypeStruct((2, 4, 8, 2, 72, 128), f32),
        ],
        scratch_shapes=[
            pltpu.VMEM((1536, 256), bf16),
            pltpu.VMEM((1536, 256), bf16),
            pltpu.VMEM((4, 256, 384), bf16),
            pltpu.VMEM((4, 256, 384), bf16),
            pltpu.VMEM((256, 128), f32),
            pltpu.VMEM((8, 256), f32),
            pltpu.VMEM((512, 1024), bf16),
            pltpu.VMEM((512, 1024), bf16),
            pltpu.VMEM((512, 1024), bf16),
            pltpu.VMEM((512, 2048), bf16),
            pltpu.VMEM((2048, 1024), bf16),
            pltpu.VMEM((4, 64, 256), f32),
        ],
        compiler_params=pltpu.CompilerParams(vmem_limit_bytes=56 << 20),
        cost_estimate=pl.CostEstimate(flops=16000000000, bytes_accessed=24 << 20, transcendentals=1 << 20),
        name="block",
    )(flag, x, wcat, wp3, bias, uhi, ulo, dohi, dolo)


def split(w):
    high = lax.reduce_precision(w, 8, 7)
    return high.astype(bf16), (w - high).astype(bf16)


def weights(gain, w_qkv, w_proj, rel_bias):
    root = 1.0 / math.sqrt(32.0)
    width = w_proj.shape[0]
    wc = gain[:, None] * w_qkv
    wc = wc * jnp.where(jnp.arange(3 * width) < width, root, 1.0)[None, :]
    wc = (wc - jnp.mean(wc, axis=0, keepdims=True)).T
    wcat = jnp.concatenate(split(wc), axis=1)
    phi, plo = split(w_proj)
    wp_rows = jnp.concatenate([phi, phi, plo], axis=0)
    wp_cols = jnp.concatenate([phi, plo, phi], axis=1)
    bias = rel_bias.reshape(4, 4, 64, 64).transpose(0, 3, 1, 2).reshape(4, 64, 256)
    return wcat, wp_rows, wp_cols, bias


def turn(size, by):
    return [(i, (i + by) % size) for i in range(size)]


def fetch(slots, plan_rank, plan_slot):
    count = lax.axis_size("buf")
    slot_count, tile_tokens, width = slots.shape[3:]
    part = tile_tokens // count
    spread = slots.reshape(slot_count, count, part, width).transpose(1, 0, 2, 3)
    held = lax.all_to_all(spread, "buf", split_axis=0, concat_axis=0, tiled=True)
    held = held.reshape(count * slot_count, part, width)
    wanted = plan_rank.reshape(count) * slot_count + plan_slot.reshape(count)
    asked = jnp.take(held, wanted, axis=0)
    return lax.all_to_all(asked, "buf", split_axis=0, concat_axis=0, tiled=True).reshape(32, 32, width)


def shift(tile):
    half = WSIDE // 2
    lat, lon = lax.axis_size("lat"), lax.axis_size("lon")
    down = lax.ppermute(tile[:half], "lat", turn(lat, -1))
    right = lax.ppermute(tile[:, :half], "lon", turn(lon, -1))
    corner_pairs = [
        (i * lon + j, (i - 1) % lat * lon + (j - 1) % lon) for i in range(lat) for j in range(lon)
    ]
    corner = lax.ppermute(tile[:half, :half], ("lat", "lon"), corner_pairs)
    top = jnp.concatenate([tile[half:, half:], right[half:]], axis=1)
    bottom = jnp.concatenate([down[:, half:], corner], axis=1)
    return jnp.concatenate([top, bottom], axis=0)


def exchange(blocks, axis, places, me, perms):
    total = lax.dynamic_index_in_dim(blocks, me, 0, keepdims=False)
    parts = []
    for by, perm in perms:
        block = lax.dynamic_index_in_dim(blocks, (me + by) % places, 0, keepdims=False)
        parts.append(lax.ppermute(block, axis, perm))
    for part in parts:
        total = total + part
    return total


def sum_bands(terms):
    buf = lax.axis_index("buf")
    core_pairs = [(i, i ^ 1) for i in range(8)]
    tail = terms.shape[-2:]
    x = exchange(terms.reshape(2, 64, *tail), "buf", 2, buf % 2, [(1, core_pairs)])
    x = x.reshape(4, 4, 4, *tail)
    x = jnp.moveaxis(x, 2, 0).reshape(4, 16, *tail)
    x = exchange(x, "lon", 4, lax.axis_index("lon"), [(d, turn(4, d)) for d in (2, 1, 3)])
    x = x.reshape(4, 4, *tail)
    x = exchange(x, "buf", 4, buf // 2, [(d, turn(8, 2 * d)) for d in (2, 1, 3)])
    return exchange(x, "lat", 4, lax.axis_index("lat"), [(d, turn(4, d)) for d in (2, 1, 3)])


def on_device(slots, plan_rank, plan_slot, gain, w_qkv, w_proj, rel_bias, cotangent):
    width = gain.shape[0]
    wcat, wp_rows, wp_cols, bias = weights(gain, w_qkv, w_proj, rel_bias)
    tokens = 128 * cotangent.shape[1] * cotangent.shape[2] * cotangent.shape[3]
    uhi, ulo, dohi, dolo = upstream_call(cotangent[0, 0], wp_cols, 1.0 / math.sqrt(tokens))
    x = shift(fetch(slots, plan_rank, plan_slot))
    last = (lax.axis_index("lat") == lax.axis_size("lat") - 1).astype(jnp.int32).reshape(1)
    output, terms = main_call(last, x, wcat, wp_rows, bias, uhi, ulo, dohi, dolo)
    band = sum_bands(terms)
    rows = band[:64].reshape(8, 2, 4, 128).transpose(2, 0, 1, 3).reshape(4, 4 * width)
    unit = rows[:, : 3 * width]
    place = (lax.axis_index("buf") * 4 + lax.axis_index("lat")) * 4 + lax.axis_index("lon")
    my_gain = lax.dynamic_slice_in_dim(gain, place * 4, 4)
    my_qkv = lax.dynamic_slice_in_dim(w_qkv, place * 4, 4)
    return (
        output.reshape(cotangent.shape),
        unit * my_gain[:, None],
        rows[:, 3 * width :],
        jnp.sum(unit * my_qkv, axis=1),
        band[64:, :64],
    )


def solution(mesh):
    placed = (
        P("buf", "lat", "lon", None, None, None),
        P("lat", "lon", None, None),
        P("lat", "lon", None),
        P(),
        P(),
        P(),
        P(),
        P("buf", None, "lat", "lon", None),
    )
    return jax.shard_map(
        on_device,
        mesh=mesh,
        in_specs=placed,
        out_specs=(
            P("buf", None, "lat", "lon", None),
            P(("buf", "lat", "lon"), None),
            P(("buf", "lat", "lon"), None),
            P(("buf", "lat", "lon")),
            P(("buf", "lat", "lon"), None),
        ),
        check_vma=False,
    )
```

```python
import functools
import math

import jax
import jax.numpy as jnp
from jax import lax
from jax.experimental import pallas as pl
from jax.experimental.pallas import tpu as pltpu
from jax.sharding import PartitionSpec as P

HEADS = 16
WSIDE = 8
NT = (((1,), (1,)), ((), ()))
NN = (((1,), (0,)), ((), ()))
f32, bf16 = jnp.float32, jnp.bfloat16


def dot(left, right, dims=NN):
    return lax.dot_general(left, right, dims, preferred_element_type=f32)


def halves(value):
    high = value.astype(bf16)
    return high, (value - high.astype(f32)).astype(bf16)


def window_rows(block):
    pieces = [block[u, 8 * w : 8 * w + 8, :] for w in range(4) for u in range(8)]
    return jnp.concatenate(pieces, axis=0)


def upstream_kernel(scale, cot_ref, wp3_ref, uhi_ref, ulo_ref, dohi_ref, dolo_ref):
    upstream = window_rows(cot_ref) * scale
    uhi, ulo = halves(upstream)
    uhi_ref[...] = uhi
    ulo_ref[...] = ulo
    u3 = jnp.concatenate([uhi, uhi, ulo], axis=1)
    for at in range(0, 512, 128):
        dohi_ref[at : at + 128, :], dolo_ref[at : at + 128, :] = halves(
            dot(wp3_ref[at : at + 128, :], u3, NT)
        )


def swap(value):
    return jnp.concatenate([value[:, 64:], value[:, :64]], axis=1)


def block_diagonal(value, left, right):
    other = swap(value)
    zeros = jnp.zeros((32, 128), bf16)
    for even, odd in ((value, other), (other, value)):
        first = jnp.concatenate([even[0:32] * left, odd[32:64] * right, zeros, zeros], axis=0)
        second = jnp.concatenate([zeros, zeros, even[64:96] * left, odd[96:128] * right], axis=0)
        yield jnp.concatenate([first, second], axis=1)


def gather_diagonal(lane, pair_a, pair_b):
    low = lane < 64
    return jnp.concatenate(
        [
            jnp.where(low, pair_a[:32], swap(pair_b[:32])),
            jnp.where(low, swap(pair_a[32:]), pair_b[32:]),
        ],
        axis=0,
    )


def heads_product(left2, hi, lo, window):
    zeros = jnp.zeros((64, 128), bf16)
    for t in range(2):
        h, l = hi[:, 128 * t : 128 * t + 128], lo[:, 128 * t : 128 * t + 128]
        right = jnp.concatenate([h, l, h, zeros] if window == 0 else [h, l, zeros, h], axis=0)
        yield dot(left2[64 * t : 64 * t + 64], right)


def main_kernel(
    flag_ref, x_ref, wcat_ref, wp3_ref, bias_ref, uhi_ref, ulo_ref, dohi_ref, dolo_ref,
    out_ref, own_ref, other_ref,
    pkhi, pklo, kt, vt, rstd_tok, rstd_lane, xt_all, ahi_all, alo_all, gq_all, gkv_all, rel_acc,
):
    step = pl.program_id(0)
    here = pl.ds(pl.multiple_of(step * 256, 256), 256)
    here_lo = pl.ds(pl.multiple_of(step * 256 + 1024, 256), 256)

    @pl.when(step == 0)
    def _():
        rel_acc[...] = jnp.zeros_like(rel_acc)

    tokens = window_rows(x_ref[...].astype(f32))
    tokens16 = tokens.astype(bf16)
    eye = (
        lax.broadcasted_iota(jnp.int32, (256, 256), 0) == lax.broadcasted_iota(jnp.int32, (256, 256), 1)
    ).astype(f32).astype(bf16)
    xt = jnp.concatenate([dot(eye, tokens16[:, :256], NT), dot(eye, tokens16[:, 256:], NT)], axis=0)
    xt16 = xt.astype(bf16)
    xt_all[:, here] = xt16
    mean = jnp.sum(xt, axis=0, keepdims=True) * (1.0 / 512)
    centered = xt - mean
    spread = jnp.sum(centered * centered, axis=0, keepdims=True) * (1.0 / 512)
    rstd = lax.rsqrt(spread + 1e-05)
    rstd_lane[...] = rstd * jnp.ones((8, 1), f32)
    rstd_tok[...] = jnp.transpose(jnp.broadcast_to(rstd, (128, 256)))
    twice = jnp.concatenate([xt16, xt16], axis=0)
    for at in range(0, 1536, 128):
        rows = slice(at, at + 128)
        pkhi[rows, :], pklo[rows, :] = halves(dot(wcat_ref[rows, :], twice) * rstd)
    for base, tok in ((512, kt), (1024, vt)):
        for g in range(4):
            rows = slice(base + 128 * g, base + 128 * g + 128)
            high = dot(eye, pkhi[rows, :], NT).astype(bf16)
            low = dot(eye, pklo[rows, :], NT).astype(bf16)
            tok[g, :, 0:128] = high
            tok[g, :, 128:256] = low
            tok[g, :, 256:384] = high

    lane = lax.broadcasted_iota(jnp.int32, (1, 128), 1)
    left16 = (lane < 64).astype(f32).astype(bf16)
    right16 = (lane >= 64).astype(f32).astype(bf16)
    edge = (flag_ref[0] > 0) & (step == 3)
    row_of = lax.broadcasted_iota(jnp.int32, (64, 256), 0)
    lane_of = lax.broadcasted_iota(jnp.int32, (64, 256), 1)
    crossing = ((row_of >= 32) != ((lane_of & 63) >= 32)) & edge
    root = 1.0 / math.sqrt(32.0)

    def operands(g):
        rows_q = pl.ds(pl.multiple_of(g * 128, 128), 128)
        rows_k = pl.ds(pl.multiple_of(g * 128 + 512, 128), 128)
        rows_v = pl.ds(pl.multiple_of(g * 128 + 1024, 128), 128)
        unit = []
        for p in range(2):
            lanes = slice(128 * p, 128 * p + 128)
            qhi = list(block_diagonal(pkhi[rows_q, lanes], left16, right16))
            qlo = list(block_diagonal(pklo[rows_q, lanes], left16, right16))
            ohi = list(block_diagonal(dohi_ref[rows_q, lanes], left16, right16))
            olo = list(block_diagonal(dolo_ref[rows_q, lanes], left16, right16))
            both = []
            for rows in (rows_k, rows_v):
                high, low = pkhi[rows, lanes], pklo[rows, lanes]
                other = swap(high)
                first = high * left16 + other * right16
                second = other * left16 + high * right16
                both.append([jnp.concatenate([first, low], axis=1), jnp.concatenate([second, low], axis=1)])
            for w in range(2):
                unit.append((qhi[w], qlo[w], ohi[w], olo[w], both[0][w], both[1][w]))
        scores, products = [], []
        for n, (qh, ql, oh, ol, _, _) in enumerate(unit):
            at = 64 * n
            scores.append(dot(kt[g, at : at + 64, :], jnp.concatenate([qh, qh, ql], axis=0)))
            products.append(dot(vt[g, at : at + 64, :], jnp.concatenate([oh, oh, ol], axis=0)))
        return unit, scores, products

    def rest(g, state):
        unit, scores, products = state
        rows_q = pl.ds(pl.multiple_of(g * 128, 128), 128)
        cols_k = rows_q
        cols_v = pl.ds(pl.multiple_of(g * 128 + 512, 128), 128)
        probs, attended, dss, grad_q = [], [], [], []
        for n in range(4):
            s = jnp.where(crossing, -1000000000.0, scores[n] + bias_ref[g])
            e = jnp.exp(s - jnp.max(s, axis=0, keepdims=True))
            weights = e * (1.0 / jnp.sum(e, axis=0, keepdims=True))
            inner = jnp.sum(weights * products[n], axis=0, keepdims=True)
            ds = weights * (products[n] - inner)
            probs.append(halves(weights))
            dss.append(ds)
        rel_acc[g] = rel_acc[g] + ((dss[0] + dss[1]) + (dss[2] + dss[3]))
        dss = [halves(ds) for ds in dss]
        for n in range(4):
            attended.append(list(heads_product(unit[n][5], *probs[n], n % 2)))
        for n in range(4):
            grad_q.append(list(heads_product(unit[n][4], *dss[n], n % 2)))
        for pairs, hi_at, cols in ((probs, 2, cols_v), (dss, 0, cols_k)):
            for n in range(4):
                at = 64 * n
                to = pl.ds(pl.multiple_of(step * 256 + at, 64), 64)
                to_lo = pl.ds(pl.multiple_of(step * 256 + at + 1024, 64), 64)
                full = dot(
                    jnp.concatenate(pairs[n], axis=0),
                    jnp.concatenate([unit[n][hi_at], unit[n][hi_at + 1]], axis=0),
                    NT,
                )
                total = full[:64, :128] + full[64:, :128] + full[:64, 128:]
                gkv_all[to, cols], gkv_all[to_lo, cols] = halves(total * rstd_tok[at : at + 64, :])
        for p in range(2):
            lanes = slice(128 * p, 128 * p + 128)
            here_p = pl.ds(pl.multiple_of(step * 256 + 128 * p, 128), 128)
            here_p_lo = pl.ds(pl.multiple_of(step * 256 + 128 * p + 1024, 128), 128)
            one, two = 2 * p, 2 * p + 1
            att = jnp.concatenate([gather_diagonal(lane, attended[one][t], attended[two][t]) for t in range(2)], axis=0)
            ahi_all[rows_q, here_p], alo_all[rows_q, here_p] = halves(att)
            gq = jnp.concatenate([gather_diagonal(lane, grad_q[one][t], grad_q[two][t]) for t in range(2)], axis=0)
            gq = gq * (rstd_lane[0:1, lanes] * root)
            gq_all[rows_q, here_p], gq_all[rows_q, here_p_lo] = halves(gq)

    def group(g, carry):
        rest(g, operands(g))
        return carry

    for g in range(4):
        group(g, 0)

    tok_hi = dot(eye, ahi_all[:, here], NT).astype(bf16)
    tok_lo = dot(eye, alo_all[:, here], NT).astype(bf16)
    result = tokens + dot(
        jnp.concatenate([tok_hi, tok_lo, tok_hi], axis=1), wp3_ref[...]
    )
    for w in range(4):
        for u in range(8):
            out_ref[u, 8 * w : 8 * w + 8, :] = result[64 * w + 8 * u : 64 * w + 8 * u + 8, :]

    @pl.when(step == 3)
    def _():
        sub = lax.broadcasted_iota(jnp.int32, (1, 8, 128), 1)
        first = flag_ref[1] == 0

        def pack(k, value):
            a, b = value[:, :128].reshape(64, 8, 128), value[:, 128:].reshape(64, 8, 128)
            aa = jnp.concatenate([a[:, 4:], a[:, :4]], axis=1)
            bb = jnp.concatenate([b[:, 4:], b[:, :4]], axis=1)
            even = jnp.where(sub < 4, a, bb).reshape(4, 2, 8, 8, 128)
            odd = jnp.where(sub < 4, aa, b).reshape(4, 2, 8, 8, 128)
            at = slice(8 * k, 8 * k + 8)
            for n, block in ((0, even), (1, odd)):
                own_ref[:, :, n, at, :] = jnp.where(first, block[:, 0], block[:, 1])
                other_ref[:, :, n, at, :] = jnp.where(first, block[:, 1], block[:, 0])

        twice = jnp.concatenate([xt_all[...], xt_all[...]], axis=1)
        for k in range(6):
            if k < 2:
                value = dot(twice, gq_all[256 * k : 256 * k + 256, :], NT)
            else:
                value = dot(twice, gkv_all[:, 256 * k - 512 : 256 * k - 256])
            pack(k, value - jnp.sum(value, axis=0, keepdims=True) * (1.0 / 512))
        for k in range(2):
            cols = slice(256 * k, 256 * k + 256)
            u = uhi_ref[:, cols]
            value = (
                dot(ahi_all[...], u) + dot(alo_all[...], u) + dot(ahi_all[...], ulo_ref[:, cols])
            )
            pack(6 + k, value)
        for g in range(4):
            turned = jnp.transpose(
                jnp.concatenate([rel_acc[g], jnp.zeros((64, 256), f32)], axis=0)
            ).reshape(2, 8, 2, 8, 128)
            own_ref[g, :, :, 64:72, :] = jnp.where(first, turned[0], turned[1])
            other_ref[g, :, :, 64:72, :] = jnp.where(first, turned[1], turned[0])


def full(shape):
    return pl.BlockSpec(shape, lambda a: (0,) * len(shape))


def once(shape):
    return pl.BlockSpec(shape, lambda a: (0,) * len(shape), pipeline_mode=pl.Buffered(1))


def upstream_call(cot, wp3, scale):
    return pl.pallas_call(
        functools.partial(upstream_kernel, scale),
        grid=(4,),
        in_specs=[pl.BlockSpec((8, 32, 512), lambda a: (a, 0, 0)), full((512, 1536))],
        out_specs=[
            pl.BlockSpec((256, 512), lambda a: (a, 0)),
            pl.BlockSpec((256, 512), lambda a: (a, 0)),
            pl.BlockSpec((512, 256), lambda a: (0, a)),
            pl.BlockSpec((512, 256), lambda a: (0, a)),
        ],
        out_shape=[jax.ShapeDtypeStruct((1024, 512), bf16)] * 2
        + [jax.ShapeDtypeStruct((512, 1024), bf16)] * 2,
        compiler_params=pltpu.CompilerParams(vmem_limit_bytes=40 << 20),
        cost_estimate=pl.CostEstimate(flops=1600000000, bytes_accessed=8 << 20, transcendentals=0),
        name="upstream",
    )(cot, wp3)


def main_call(flag, x, wcat, wp3, bias, uhi, ulo, dohi, dolo):
    return pl.pallas_call(
        main_kernel,
        grid=(4,),
        in_specs=[
            pl.BlockSpec(memory_space=pltpu.SMEM),
            pl.BlockSpec((8, 32, 512), lambda a: (a, 0, 0)),
            once((1536, 1024)),
            once((1536, 512)),
            once((4, 64, 256)),
            once((1024, 512)),
            once((1024, 512)),
            pl.BlockSpec((512, 256), lambda a: (0, a)),
            pl.BlockSpec((512, 256), lambda a: (0, a)),
        ],
        out_specs=[
            pl.BlockSpec((8, 32, 512), lambda a: (a, 0, 0)),
            once((4, 8, 2, 72, 128)),
            once((4, 8, 2, 72, 128)),
        ],
        out_shape=[
            jax.ShapeDtypeStruct((32, 32, 512), f32),
            jax.ShapeDtypeStruct((4, 8, 2, 72, 128), f32),
            jax.ShapeDtypeStruct((4, 8, 2, 72, 128), f32),
        ],
        scratch_shapes=[
            pltpu.VMEM((1536, 256), bf16),
            pltpu.VMEM((1536, 256), bf16),
            pltpu.VMEM((4, 256, 384), bf16),
            pltpu.VMEM((4, 256, 384), bf16),
            pltpu.VMEM((256, 128), f32),
            pltpu.VMEM((8, 256), f32),
            pltpu.VMEM((512, 1024), bf16),
            pltpu.VMEM((512, 1024), bf16),
            pltpu.VMEM((512, 1024), bf16),
            pltpu.VMEM((512, 2048), bf16),
            pltpu.VMEM((2048, 1024), bf16),
            pltpu.VMEM((4, 64, 256), f32),
        ],
        compiler_params=pltpu.CompilerParams(vmem_limit_bytes=40 << 20),
        cost_estimate=pl.CostEstimate(flops=16000000000, bytes_accessed=24 << 20, transcendentals=1 << 20),
        name="block",
    )(flag, x, wcat, wp3, bias, uhi, ulo, dohi, dolo)


def split(w):
    high = lax.reduce_precision(w, 8, 7)
    return high.astype(bf16), (w - high).astype(bf16)


def weights(gain, w_qkv, w_proj, rel_bias):
    root = 1.0 / math.sqrt(32.0)
    width = w_proj.shape[0]
    wc = gain[:, None] * w_qkv
    wc = wc * jnp.where(jnp.arange(3 * width) < width, root, 1.0)[None, :]
    wc = (wc - jnp.mean(wc, axis=0, keepdims=True)).T
    wcat = jnp.concatenate(split(wc), axis=1)
    phi, plo = split(w_proj)
    wp_rows = jnp.concatenate([phi, phi, plo], axis=0)
    wp_cols = jnp.concatenate([phi, plo, phi], axis=1)
    bias = rel_bias.reshape(4, 4, 64, 64).transpose(0, 3, 1, 2).reshape(4, 64, 256)
    return wcat, wp_rows, wp_cols, bias


def turn(size, by):
    return [(i, (i + by) % size) for i in range(size)]


def fetch(slots, plan_rank, plan_slot, ready):
    count = lax.axis_size("buf")
    slot_count, tile_tokens, width = slots.shape[3:]
    part = tile_tokens // count
    spread = slots.reshape(slot_count, count, part, width).transpose(1, 0, 2, 3)
    held = lax.all_to_all(spread, "buf", split_axis=0, concat_axis=0, tiled=True)
    held, ready = lax.optimization_barrier((held, ready))
    held = held.reshape(count * slot_count, part, width)
    wanted = plan_rank.reshape(count) * slot_count + plan_slot.reshape(count)
    asked = jnp.take(held, wanted, axis=0)
    tile = lax.all_to_all(asked, "buf", split_axis=0, concat_axis=0, tiled=True)
    return tile.reshape(32, 32, width), ready


def shift(tile):
    half = WSIDE // 2
    lat, lon = lax.axis_size("lat"), lax.axis_size("lon")
    down = lax.ppermute(tile[:half], "lat", turn(lat, -1))
    right = lax.ppermute(tile[:, :half], "lon", turn(lon, -1))
    corner_pairs = [
        (i * lon + j, (i - 1) % lat * lon + (j - 1) % lon) for i in range(lat) for j in range(lon)
    ]
    corner = lax.ppermute(tile[:half, :half], ("lat", "lon"), corner_pairs)
    top = jnp.concatenate([tile[half:, half:], right[half:]], axis=1)
    bottom = jnp.concatenate([down[:, half:], corner], axis=1)
    return jnp.concatenate([top, bottom], axis=0)


def exchange(blocks, axis, places, me, perms):
    total = lax.dynamic_index_in_dim(blocks, me, 0, keepdims=False)
    parts = []
    for by, perm in perms:
        block = lax.dynamic_index_in_dim(blocks, (me + by) % places, 0, keepdims=False)
        parts.append(lax.ppermute(block, axis, perm))
    for part in parts:
        total = total + part
    return total


def sum_bands(own, other):
    buf, lat, lon = lax.axis_index("buf"), lax.axis_index("lat"), lax.axis_index("lon")
    x = own + lax.ppermute(other, "buf", [(i, i ^ 1) for i in range(8)])
    x = x.reshape(4, 4, 4, 72, 128)
    ring = [(d, turn(4, d)) for d in (2, 1, 3)]
    left = exchange(jnp.moveaxis(x[..., :40, :], 2, 0), "lon", 4, lon, ring)
    right = exchange(jnp.moveaxis(x[..., 40:, :], 1, 0), "lat", 4, lat, ring)
    left = exchange(jnp.moveaxis(left, 1, 0), "lat", 4, lat, ring)
    right = exchange(jnp.moveaxis(right, 1, 0), "lon", 4, lon, ring)
    x = jnp.concatenate([left, right], axis=1)
    return exchange(x, "buf", 4, buf // 2, [(d, turn(8, 2 * d)) for d in (2, 1, 3)])


def on_device(slots, plan_rank, plan_slot, gain, w_qkv, w_proj, rel_bias, cotangent):
    width = gain.shape[0]
    wcat, wp_rows, wp_cols, bias = weights(gain, w_qkv, w_proj, rel_bias)
    tokens = 128 * cotangent.shape[1] * cotangent.shape[2] * cotangent.shape[3]
    ready = upstream_call(cotangent[0, 0], wp_cols, 1.0 / math.sqrt(tokens))
    tile, ready = fetch(slots, plan_rank, plan_slot, (wcat, wp_rows, bias, *ready))
    x = shift(tile)
    last = lax.axis_index("lat") == lax.axis_size("lat") - 1
    flags = jnp.stack([last.astype(jnp.int32), lax.axis_index("buf") % 2])
    output, own, other = main_call(flags, x, *ready)
    band = sum_bands(own, other)
    rows = band[:64].reshape(8, 2, 4, 128).transpose(2, 0, 1, 3).reshape(4, 4 * width)
    unit = rows[:, : 3 * width]
    place = (lax.axis_index("buf") * 4 + lax.axis_index("lat")) * 4 + lax.axis_index("lon")
    my_gain = lax.dynamic_slice_in_dim(gain, place * 4, 4)
    my_qkv = lax.dynamic_slice_in_dim(w_qkv, place * 4, 4)
    return (
        output.reshape(cotangent.shape),
        unit * my_gain[:, None],
        rows[:, 3 * width :],
        jnp.sum(unit * my_qkv, axis=1),
        band[64:, :64],
    )


def solution(mesh):
    placed = (
        P("buf", "lat", "lon", None, None, None),
        P("lat", "lon", None, None),
        P("lat", "lon", None),
        P(),
        P(),
        P(),
        P(),
        P("buf", None, "lat", "lon", None),
    )
    return jax.shard_map(
        on_device,
        mesh=mesh,
        in_specs=placed,
        out_specs=(
            P("buf", None, "lat", "lon", None),
            P(("buf", "lat", "lon"), None),
            P(("buf", "lat", "lon"), None),
            P(("buf", "lat", "lon")),
            P(("buf", "lat", "lon"), None),
        ),
        check_vma=False,
    )
```

```python
import functools
import math

import jax
import jax.numpy as jnp
from jax import lax
from jax.experimental import pallas as pl
from jax.experimental.pallas import tpu as pltpu
from jax.sharding import PartitionSpec as P

HEADS = 16
WSIDE = 8
NT = (((1,), (1,)), ((), ()))
NN = (((1,), (0,)), ((), ()))
f32, bf16 = jnp.float32, jnp.bfloat16


def dot(left, right, dims=NN):
    return lax.dot_general(left, right, dims, preferred_element_type=f32)


def halves(value):
    high = value.astype(bf16)
    return high, (value - high.astype(f32)).astype(bf16)


def window_rows(block):
    pieces = [block[u, 8 * w : 8 * w + 8, :] for w in range(4) for u in range(8)]
    return jnp.concatenate(pieces, axis=0)


def upstream_kernel(scale, cot_ref, wp3_ref, uhi_ref, ulo_ref, dohi_ref, dolo_ref, dotok_ref):
    upstream = window_rows(cot_ref) * scale
    uhi, ulo = halves(upstream)
    uhi_ref[...] = uhi
    ulo_ref[...] = ulo
    u3 = jnp.concatenate([uhi, uhi, ulo], axis=1)
    for at in range(0, 512, 128):
        hi, lo = halves(dot(wp3_ref[at : at + 128, :], u3, NT))
        dohi_ref[at : at + 128, :], dolo_ref[at : at + 128, :] = hi, lo
        dotok_ref[:, 2 * at : 2 * at + 128] = hi.T
        dotok_ref[:, 2 * at + 128 : 2 * at + 256] = lo.T


def swap(value):
    return jnp.concatenate([value[:, 64:], value[:, :64]], axis=1)


def block_diagonal(value, left, right):
    other = swap(value)
    zeros = jnp.zeros((32, 128), bf16)
    for even, odd in ((value, other), (other, value)):
        first = jnp.concatenate([even[0:32] * left, odd[32:64] * right, zeros, zeros], axis=0)
        second = jnp.concatenate([zeros, zeros, even[64:96] * left, odd[96:128] * right], axis=0)
        yield jnp.concatenate([first, second], axis=1)


def gather_diagonal(lane, pair_a, pair_b):
    low = lane < 64
    return jnp.concatenate(
        [
            jnp.where(low, pair_a[:32], swap(pair_b[:32])),
            jnp.where(low, swap(pair_a[32:]), pair_b[32:]),
        ],
        axis=0,
    )


def heads_product(left2, hi, lo, window):
    zeros = jnp.zeros((64, 256), bf16)
    right = jnp.concatenate([hi, lo, hi, zeros] if window == 0 else [hi, lo, zeros, hi], axis=0)
    product = dot(left2, right)
    return [product[:64, :128], product[64:, 128:]]


def fill(source, step, slot, wcat, xt_all):
    pkhi, pklo, kt, vt, rstd_tok, rstd_lane, qt = slot
    here = pl.ds(pl.multiple_of(step * 256, 256), 256)
    kept = {}

    def project(first):
        for at in range(first, first + 512, 128):
            rows = slice(at, at + 128)
            pkhi[rows, :], pklo[rows, :] = halves(dot(wcat[rows, :], kept["twice"]) * kept["rstd"])

    def turned(base, tok):
        for g in range(4):
            rows = slice(base + 128 * g, base + 128 * g + 128)
            high = pkhi[rows, :].T
            tok[g, :, 0:128] = high
            tok[g, :, 128:256] = pklo[rows, :].T
            if base:
                tok[g, :, 256:384] = high

    def begin():
        tile, side, x_all = source
        rows = [tile[step * 8 + 4 + u].astype(f32) for u in range(8)]
        ends = [side[step * 8 + 4 + u].astype(f32) for u in range(8)]
        pieces = []
        for w in range(4):
            for u in range(8):
                if w < 3:
                    pieces.append(rows[u][8 * w + 4 : 8 * w + 12])
                else:
                    pieces.append(jnp.concatenate([rows[u][28:], ends[u]], axis=0))
        tokens16 = jnp.concatenate(pieces, axis=0).astype(bf16)
        x_all[here, :] = tokens16
        xt = tokens16.T.astype(f32)
        xt16 = xt.astype(bf16)
        xt_all[:, here] = xt16
        mean = jnp.sum(xt, axis=0, keepdims=True) * (1.0 / 512)
        centered = xt - mean
        spread = jnp.sum(centered * centered, axis=0, keepdims=True) * (1.0 / 512)
        rstd = lax.rsqrt(spread + 1e-05)
        rstd_lane[...] = rstd * jnp.ones((8, 1), f32)
        rstd_tok[...] = jnp.transpose(jnp.broadcast_to(rstd, (128, 256)))
        kept["rstd"] = rstd
        kept["twice"] = jnp.concatenate([xt16, xt16], axis=0)

    def queries():
        project(0)
        turned(0, qt)

    def keys():
        project(512)
        turned(512, kt)

    def values():
        project(1024)
        turned(1024, vt)

    return [begin, queries, keys, values]


def main_kernel(
    flag_ref, tile_hbm, down_hbm, right_hbm, corner_hbm, wcat_hbm, bias_hbm, uhi_hbm, ulo_hbm, dohi_ref, dolo_ref, dotok_ref,
    own_hbm, other_hbm, ahi_ref, alo_ref, x_hbm,
    pkhi0, pklo0, kt0, vt0, rt0, rl0, qt0, pkhi1, pklo1, kt1, vt1, rt1, rl1, qt1,
    xt_all, ahi_all, alo_all, g_all, rel_acc,
    wcat, bias_ref, uhi_ref, ulo_ref, own_ref, other_ref, tile, side, x_all, in_sem, out_sem,
):
    step = pl.program_id(0)
    slots = ((pkhi0, pklo0, kt0, vt0, rt0, rl0, qt0), (pkhi1, pklo1, kt1, vt1, rt1, rl1, qt1))
    loads = [
        pltpu.make_async_copy(source, target, in_sem.at[n])
        for n, (source, target) in enumerate(
            (
                (tile_hbm, tile.at[:32]),
                (down_hbm, tile.at[32:]),
                (right_hbm, side.at[:32]),
                (corner_hbm, side.at[32:]),
                (wcat_hbm, wcat),
                (bias_hbm, bias_ref),
                (uhi_hbm, uhi_ref),
                (ulo_hbm, ulo_ref),
            )
        )
    ]
    source = (tile, side, x_all)
    lane = lax.broadcasted_iota(jnp.int32, (1, 128), 1)
    left16 = (lane < 64).astype(f32).astype(bf16)
    right16 = (lane >= 64).astype(f32).astype(bf16)
    lane2 = lax.broadcasted_iota(jnp.int32, (1, 256), 1) & 127
    head_of = [((lane2 >= 32 * j) & (lane2 < 32 * j + 32)).astype(f32).astype(bf16) for j in range(4)]
    row_of = lax.broadcasted_iota(jnp.int32, (64, 256), 0)
    lane_of = lax.broadcasted_iota(jnp.int32, (64, 256), 1)
    root = 1.0 / math.sqrt(32.0)

    def operands(g, slot):
        pkhi, pklo, kt, vt = slot[:4]
        rows_q, rows_k, rows_v = (slice(128 * g + base, 128 * g + base + 128) for base in (0, 512, 1024))
        unit = []
        for p in range(2):
            lanes = slice(128 * p, 128 * p + 128)
            qhi = list(block_diagonal(pkhi[rows_q, lanes], left16, right16))
            qlo = list(block_diagonal(pklo[rows_q, lanes], left16, right16))
            ohi = list(block_diagonal(dohi_ref[rows_q, lanes], left16, right16))
            olo = list(block_diagonal(dolo_ref[rows_q, lanes], left16, right16))
            both = []
            for rows in (rows_k, rows_v):
                high, low = pkhi[rows, lanes], pklo[rows, lanes]
                other = swap(high)
                one = high * left16 + other * right16
                two = other * left16 + high * right16
                both.append([jnp.concatenate([one, low], axis=1), jnp.concatenate([two, low], axis=1)])
            for w in range(2):
                unit.append((qhi[w], qlo[w], ohi[w], olo[w], both[0][w], both[1][w]))
        scores, products = [], []
        for n, (qh, ql, oh, ol, _, _) in enumerate(unit):
            at = 64 * n
            scores.append(dot(kt[g, at : at + 64, :], jnp.concatenate([qh, qh, ql], axis=0)))
            products.append(dot(vt[g, at : at + 64, :], jnp.concatenate([oh, oh, ol], axis=0)))
        return unit, scores, products

    def finish(g, state, slot, edge):
        unit, scores, products = state
        rstd_tok, rstd_lane, qt = slot[4:]
        rows_q = slice(128 * g, 128 * g + 128)
        cols_k = slice(128 * g + 512, 128 * g + 640)
        cols_v = slice(128 * g + 1024, 128 * g + 1152)
        probs, attended, dss, grad_q = [], [], [], []
        for n in range(4):
            s = scores[n] + bias_ref[g]
            if edge is not None:
                s = jnp.where(edge, -1000000000.0, s)
            e = jnp.exp(s - jnp.max(s, axis=0, keepdims=True))
            weights = e * (1.0 / jnp.sum(e, axis=0, keepdims=True))
            inner = jnp.sum(weights * products[n], axis=0, keepdims=True)
            probs.append(halves(weights))
            dss.append(weights * (products[n] - inner))
        rel_acc[g] = rel_acc[g] + ((dss[0] + dss[1]) + (dss[2] + dss[3]))
        dss = [halves(ds) for ds in dss]
        for n in range(4):
            attended.append(heads_product(unit[n][5], *probs[n], n % 2))
        for n in range(4):
            grad_q.append(heads_product(unit[n][4], *dss[n], n % 2))
        for pairs, tok, cols in ((probs, None, cols_v), (dss, qt, cols_k)):
            for n in range(4):
                at = 64 * n
                if tok is None:
                    both = dotok_ref[at : at + 64, 256 * g : 256 * g + 256]
                else:
                    both = tok[g, at : at + 64, :]
                to = pl.ds(pl.multiple_of(step * 256 + at, 64), 64)
                to_lo = pl.ds(pl.multiple_of(step * 256 + at + 1024, 64), 64)
                product = dot(
                    jnp.concatenate(pairs[n], axis=0),
                    jnp.concatenate([both * mask for mask in head_of], axis=0),
                )
                total = product[:64, :128] + product[64:, :128] + product[:64, 128:]
                g_all[to, cols], g_all[to_lo, cols] = halves(total * rstd_tok[at : at + 64, :])
        for p in range(2):
            lanes = slice(128 * p, 128 * p + 128)
            here_p = pl.ds(pl.multiple_of(step * 256 + 128 * p, 128), 128)
            here_p_lo = pl.ds(pl.multiple_of(step * 256 + 128 * p + 1024, 128), 128)
            one, two = 2 * p, 2 * p + 1
            att = jnp.concatenate([gather_diagonal(lane, attended[one][t], attended[two][t]) for t in range(2)], axis=0)
            att_hi, att_lo = halves(att)
            ahi_all[rows_q, here_p], alo_all[rows_q, here_p] = att_hi, att_lo
            ahi_ref[rows_q, lanes], alo_ref[rows_q, lanes] = att_hi, att_lo
            gq = jnp.concatenate([gather_diagonal(lane, grad_q[one][t], grad_q[two][t]) for t in range(2)], axis=0)
            gq = gq * (rstd_lane[0:1, lanes] * root)
            gq_hi, gq_lo = halves(gq)
            g_all[here_p, rows_q], g_all[here_p_lo, rows_q] = gq_hi.T, gq_lo.T

    def attention(slot, beside, edge):
        state = operands(0, slot)
        for g in range(4):
            if beside is not None:
                beside[g]()
            after = operands(g + 1, slot) if g < 3 else None
            finish(g, state, slot, edge)
            state = after

    @pl.when(step == 0)
    def _():
        for load in loads:
            load.start()
        rel_acc[...] = jnp.zeros_like(rel_acc)
        parts = fill(source, 0, slots[0], wcat, xt_all)
        for load in loads[:4]:
            load.wait()
        parts[0]()
        loads[4].wait()
        for part in parts[1:]:
            part()
        loads[5].wait()

    @pl.when(step % 2 == 0)
    def _():
        attention(slots[0], fill(source, step + 1, slots[1], wcat, xt_all), None)

    @pl.when(step == 1)
    def _():
        attention(slots[1], fill(source, step + 1, slots[0], wcat, xt_all), None)

    @pl.when(step == 3)
    def _():
        keep = pltpu.make_async_copy(x_all, x_hbm, in_sem.at[8])
        keep.start()
        crossing = ((row_of >= 32) != ((lane_of & 63) >= 32)) & (flag_ref[0] > 0)
        attention(slots[1], None, crossing)
        loads[6].wait()
        loads[7].wait()
        sub = lax.broadcasted_iota(jnp.int32, (1, 8, 128), 1)
        first = flag_ref[1] == 0
        stores = [keep]

        def send(k):
            at = pl.ds(8 * k, 8)
            for n, (source, target) in enumerate(((own_ref, own_hbm), (other_ref, other_hbm))):
                copy = pltpu.make_async_copy(
                    source.at[:, :, :, at, :], target.at[:, :, :, at, :], out_sem.at[n, k]
                )
                copy.start()
                stores.append(copy)

        def pack(k, value):
            a, b = value[:, :128].reshape(64, 8, 128), value[:, 128:].reshape(64, 8, 128)
            aa = jnp.concatenate([a[:, 4:], a[:, :4]], axis=1)
            bb = jnp.concatenate([b[:, 4:], b[:, :4]], axis=1)
            even = jnp.where(sub < 4, a, bb).reshape(4, 2, 8, 8, 128)
            odd = jnp.where(sub < 4, aa, b).reshape(4, 2, 8, 8, 128)
            at = slice(8 * k, 8 * k + 8)
            for n, block in ((0, even), (1, odd)):
                own_ref[:, :, n, at, :] = jnp.where(first, block[:, 0], block[:, 1])
                other_ref[:, :, n, at, :] = jnp.where(first, block[:, 1], block[:, 0])
            send(k)

        twice = jnp.concatenate([xt_all[...], xt_all[...]], axis=1)
        for k in range(6):
            value = dot(twice, g_all[:, 256 * k : 256 * k + 256])
            pack(k, value - jnp.sum(value, axis=0, keepdims=True) * (1.0 / 512))
        for k in range(2):
            cols = slice(256 * k, 256 * k + 256)
            u = uhi_ref[:, cols]
            value = (
                dot(ahi_all[...], u) + dot(alo_all[...], u) + dot(ahi_all[...], ulo_ref[:, cols])
            )
            pack(6 + k, value)
        for g in range(4):
            turned = jnp.transpose(
                jnp.concatenate([rel_acc[g], jnp.zeros((64, 256), f32)], axis=0)
            ).reshape(2, 8, 2, 8, 128)
            own_ref[g, :, :, 64:72, :] = jnp.where(first, turned[0], turned[1])
            other_ref[g, :, :, 64:72, :] = jnp.where(first, turned[1], turned[0])
        send(8)
        for store in stores:
            store.wait()


def output_kernel(x_ref, ahi_ref, alo_ref, wp3_ref, out_ref):
    tokens = x_ref[...].astype(f32)
    tok_hi, tok_lo = ahi_ref[...].T, alo_ref[...].T
    result = tokens + dot(jnp.concatenate([tok_hi, tok_lo, tok_hi], axis=1), wp3_ref[...])
    for w in range(4):
        for u in range(8):
            out_ref[u, 8 * w : 8 * w + 8, :] = result[64 * w + 8 * u : 64 * w + 8 * u + 8, :]


def full(shape):
    return pl.BlockSpec(shape, lambda a: (0,) * len(shape))


def once(shape):
    return pl.BlockSpec(shape, lambda a: (0,) * len(shape), pipeline_mode=pl.Buffered(1))


def upstream_call(cot, wp3, scale):
    return pl.pallas_call(
        functools.partial(upstream_kernel, scale),
        grid=(4,),
        in_specs=[pl.BlockSpec((8, 32, 512), lambda a: (a, 0, 0)), full((512, 1536))],
        out_specs=[
            pl.BlockSpec((256, 512), lambda a: (a, 0)),
            pl.BlockSpec((256, 512), lambda a: (a, 0)),
            pl.BlockSpec((512, 256), lambda a: (0, a)),
            pl.BlockSpec((512, 256), lambda a: (0, a)),
            pl.BlockSpec((256, 1024), lambda a: (a, 0)),
        ],
        out_shape=[jax.ShapeDtypeStruct((1024, 512), bf16)] * 2
        + [jax.ShapeDtypeStruct((512, 1024), bf16)] * 2
        + [jax.ShapeDtypeStruct((1024, 1024), bf16)],
        compiler_params=pltpu.CompilerParams(vmem_limit_bytes=24 << 20),
        cost_estimate=pl.CostEstimate(flops=1600000000, bytes_accessed=8 << 20, transcendentals=0),
        name="upstream",
    )(cot, wp3)


def main_call(flags, tile, down, right, corner, wcat, bias, uhi, ulo, dohi, dolo, dotok):
    anywhere = pl.BlockSpec(memory_space=pl.ANY)
    column = pl.BlockSpec((512, 256), lambda a: (0, a))
    slot = [
        pltpu.VMEM((1536, 256), bf16),
        pltpu.VMEM((1536, 256), bf16),
        pltpu.VMEM((4, 256, 384), bf16),
        pltpu.VMEM((4, 256, 384), bf16),
        pltpu.VMEM((256, 128), f32),
        pltpu.VMEM((8, 256), f32),
        pltpu.VMEM((4, 256, 256), bf16),
    ]
    terms = (4, 8, 2, 72, 128)
    return pl.pallas_call(
        main_kernel,
        grid=(4,),
        in_specs=[pl.BlockSpec(memory_space=pltpu.SMEM)]
        + [anywhere] * 8
        + [column] * 2
        + [pl.BlockSpec((256, 1024), lambda a: (a, 0))],
        out_specs=[anywhere] * 2 + [column] * 2 + [anywhere],
        out_shape=[jax.ShapeDtypeStruct(terms, f32)] * 2
        + [jax.ShapeDtypeStruct((512, 1024), bf16)] * 2
        + [jax.ShapeDtypeStruct((1024, 512), bf16)],
        scratch_shapes=slot
        + slot
        + [
            pltpu.VMEM((512, 1024), bf16),
            pltpu.VMEM((512, 1024), bf16),
            pltpu.VMEM((512, 1024), bf16),
            pltpu.VMEM((2048, 1536), bf16),
            pltpu.VMEM((4, 64, 256), f32),
            pltpu.VMEM((1536, 1024), bf16),
            pltpu.VMEM((4, 64, 256), f32),
            pltpu.VMEM((1024, 512), bf16),
            pltpu.VMEM((1024, 512), bf16),
            pltpu.VMEM(terms, f32),
            pltpu.VMEM(terms, f32),
            pltpu.VMEM((36, 32, 512), bf16),
            pltpu.VMEM((36, 4, 512), bf16),
            pltpu.VMEM((1024, 512), bf16),
            pltpu.SemaphoreType.DMA((9,)),
            pltpu.SemaphoreType.DMA((2, 9)),
        ],
        compiler_params=pltpu.CompilerParams(vmem_limit_bytes=56 << 20),
        cost_estimate=pl.CostEstimate(flops=16000000000, bytes_accessed=24 << 20, transcendentals=1 << 20),
        name="block",
    )(flags, tile, down, right, corner, wcat, bias, uhi, ulo, dohi, dolo, dotok)


def output_call(x, ahi, alo, wp3):
    column = pl.BlockSpec((512, 256), lambda a: (0, a))
    return pl.pallas_call(
        output_kernel,
        grid=(4,),
        in_specs=[pl.BlockSpec((256, 512), lambda a: (a, 0)), column, column, once((1536, 512))],
        out_specs=pl.BlockSpec((8, 32, 512), lambda a: (a, 0, 0)),
        out_shape=jax.ShapeDtypeStruct((32, 32, 512), f32),
        compiler_params=pltpu.CompilerParams(vmem_limit_bytes=56 << 20),
        cost_estimate=pl.CostEstimate(flops=1600000000, bytes_accessed=8 << 20, transcendentals=0),
        name="output",
    )(x, ahi, alo, wp3)


def split(w):
    high = lax.reduce_precision(w, 8, 7)
    return high.astype(bf16), (w - high).astype(bf16)


def weights(gain, w_qkv, w_proj, rel_bias):
    root = 1.0 / math.sqrt(32.0)
    width = w_proj.shape[0]
    wc = gain[:, None] * w_qkv
    wc = wc * jnp.where(jnp.arange(3 * width) < width, root, 1.0)[None, :]
    wc = (wc - jnp.mean(wc, axis=0, keepdims=True)).T
    wcat = jnp.concatenate(split(wc), axis=1)
    phi, plo = split(w_proj)
    wp_rows = jnp.concatenate([phi, phi, plo], axis=0)
    wp_cols = jnp.concatenate([phi, plo, phi], axis=1)
    bias = rel_bias.reshape(4, 4, 64, 64).transpose(0, 3, 1, 2).reshape(4, 64, 256)
    return wcat, wp_rows, wp_cols, bias


ORDER = (0, 2, 1, 3)


def band_kernel(a_ref, b_ref, c_ref, d_ref, gain_ref, rows_ref, qkv_ref, proj_ref, gain_out, rel_ref):
    total = (a_ref[...] + b_ref[...]) + (c_ref[...] + d_ref[...])
    gain = gain_ref[...]
    sums = jnp.zeros((4, 128), f32)
    for k in range(12):
        part = total[4 * k : 4 * k + 4]
        cols = slice(128 * k, 128 * k + 128)
        qkv_ref[:, cols] = part * gain
        sums = sums + part * rows_ref[:, cols]
    for k in range(4):
        proj_ref[:, 128 * k : 128 * k + 128] = total[48 + 4 * k : 52 + 4 * k]
    rel_ref[...] = total[64:, :64]
    column = jnp.sum(sums, axis=1, keepdims=True)
    for n in range(4):
        gain_out[n] = column[n, 0]


def band_call(parts, gain, rows):
    return pl.pallas_call(
        band_kernel,
        out_shape=[
            jax.ShapeDtypeStruct((4, 1536), f32),
            jax.ShapeDtypeStruct((4, 512), f32),
            jax.ShapeDtypeStruct((4,), f32),
            jax.ShapeDtypeStruct((8, 64), f32),
        ],
        out_specs=[pl.BlockSpec(memory_space=pltpu.VMEM)] * 2
        + [pl.BlockSpec(memory_space=pltpu.SMEM), pl.BlockSpec(memory_space=pltpu.VMEM)],
        name="band",
    )(*parts, gain, rows)


def turn(size, by):
    return [(i, (i + by) % size) for i in range(size)]


def fetch(slots, plan_rank, plan_slot, early):
    count = lax.axis_size("buf")
    slot_count, tile_tokens, width = slots.shape[3:]
    part = tile_tokens // count
    spread = slots.reshape(slot_count, count, part, width).transpose(1, 0, 2, 3)
    held = lax.all_to_all(spread, "buf", split_axis=0, concat_axis=0, tiled=True)
    held, early = lax.optimization_barrier((held, early))
    held = held.reshape(count * slot_count, part, width)
    wanted = plan_rank.reshape(count) * slot_count + plan_slot.reshape(count)
    asked = held.at[wanted].get(mode="promise_in_bounds")
    tile = lax.all_to_all(asked, "buf", split_axis=0, concat_axis=0, tiled=True)
    return tile.reshape(32, 32, width), early


def edge_kernel(top_ref, side_ref, down_ref, right_ref, corner_ref):
    half = WSIDE // 2
    down_ref[...] = top_ref[...]
    right_ref[...] = side_ref[:, :half, :]
    corner_ref[...] = top_ref[:, :half, :]


def edge_call(tile):
    half, rows, width = WSIDE // 2, tile.shape[0], tile.shape[-1]
    return pl.pallas_call(
        edge_kernel,
        grid=(1,),
        in_specs=[
            pl.BlockSpec((half, rows, width), lambda a: (0, 0, 0)),
            pl.BlockSpec((rows, 16, width), lambda a: (0, 0, 0)),
        ],
        out_specs=[full((half, rows, width)), full((rows, half, width)), full((half, half, width))],
        out_shape=[
            jax.ShapeDtypeStruct(shape, bf16)
            for shape in ((half, rows, width), (rows, half, width), (half, half, width))
        ],
        compiler_params=pltpu.CompilerParams(vmem_limit_bytes=56 << 20),
        name="edges",
    )(tile, tile)


def halo(tile):
    lat, lon = lax.axis_size("lat"), lax.axis_size("lon")
    down, right, corner = edge_call(tile)
    down = lax.ppermute(down, "lat", turn(lat, -1))
    right = lax.ppermute(right, "lon", turn(lon, -1))
    corner_pairs = [
        (i * lon + j, (i - 1) % lat * lon + (j - 1) % lon) for i in range(lat) for j in range(lon)
    ]
    corner = lax.ppermute(corner, ("lat", "lon"), corner_pairs)
    return tile, down, right, corner


def send(blocks, axis, size, step):
    moved = [lax.ppermute(b, axis, turn(size, step * by)) for b, by in zip(blocks[1:], ORDER[1:])]
    return [blocks[0], *moved]


def choose(blocks, me):
    return [lax.dynamic_index_in_dim(blocks, (me + by) % 4, 0, keepdims=False) for by in ORDER]


def total(parts):
    return (parts[0] + parts[1]) + (parts[2] + parts[3])


def sum_bands(own, other, work):
    buf, lat, lon = lax.axis_index("buf"), lax.axis_index("lat"), lax.axis_index("lon")
    got = lax.ppermute(other, "buf", [(i, i ^ 1) for i in range(8)])
    got, output = lax.optimization_barrier((got, work()))
    x = (own + got).reshape(4, 4, 4, 72, 128)
    left = total(send(choose(jnp.moveaxis(x[..., :40, :], 2, 0), lon), "lon", 4, 1))
    right = total(send(choose(jnp.moveaxis(x[..., 40:, :], 1, 0), lat), "lat", 4, 1))
    left = total(send(choose(jnp.moveaxis(left, 1, 0), lat), "lat", 4, 1))
    right = total(send(choose(jnp.moveaxis(right, 1, 0), lon), "lon", 4, 1))
    return output, send(choose(jnp.concatenate([left, right], axis=1), buf // 2), "buf", 8, 2)


def on_device(slots, plan_rank, plan_slot, gain, w_qkv, w_proj, rel_bias, cotangent):
    width = gain.shape[0]
    wcat, wp_rows, wp_cols, bias = weights(gain, w_qkv, w_proj, rel_bias)
    tokens = 128 * cotangent.shape[1] * cotangent.shape[2] * cotangent.shape[3]
    ready = upstream_call(cotangent[0, 0], wp_cols, 1.0 / math.sqrt(tokens))
    place = (lax.axis_index("buf") * 4 + lax.axis_index("lat")) * 4 + lax.axis_index("lon")
    my_gain = jnp.broadcast_to(lax.dynamic_slice_in_dim(gain, place * 4, 4)[:, None], (4, 128))
    my_rows = lax.dynamic_slice_in_dim(w_qkv, place * 4, 4)
    last = lax.axis_index("lat") == lax.axis_size("lat") - 1
    flags = jnp.stack([last.astype(jnp.int32), lax.axis_index("buf") % 2])
    early = (ready, bias, wp_rows, wcat, my_gain, my_rows, flags)
    tile, early = fetch(slots, plan_rank, plan_slot, early)
    ready, bias, wp_rows, wcat, my_gain, my_rows, flags = early
    own, other, ahi, alo, x = main_call(flags, *halo(tile), wcat, bias, *ready)
    output, parts = sum_bands(own, other, lambda: output_call(x, ahi, alo, wp_rows))
    grad_qkv, grad_proj, grad_gain, grad_rel = band_call(parts, my_gain, my_rows)
    return (output.reshape(cotangent.shape), grad_qkv, grad_proj, grad_gain, grad_rel)


def solution(mesh):
    placed = (
        P("buf", "lat", "lon", None, None, None),
        P("lat", "lon", None, None),
        P("lat", "lon", None),
        P(),
        P(),
        P(),
        P(),
        P("buf", None, "lat", "lon", None),
    )
    return jax.shard_map(
        on_device,
        mesh=mesh,
        in_specs=placed,
        out_specs=(
            P("buf", None, "lat", "lon", None),
            P(("buf", "lat", "lon"), None),
            P(("buf", "lat", "lon"), None),
            P(("buf", "lat", "lon")),
            P(("buf", "lat", "lon"), None),
        ),
        check_vma=False,
    )
```

```python
import functools
import math

import jax
import jax.numpy as jnp
from jax import lax
from jax.experimental import pallas as pl
from jax.experimental.pallas import tpu as pltpu
from jax.sharding import PartitionSpec as P

HEADS = 16
WSIDE = 8
NT = (((1,), (1,)), ((), ()))
NN = (((1,), (0,)), ((), ()))
f32, bf16 = jnp.float32, jnp.bfloat16


def dot(left, right, dims=NN):
    return lax.dot_general(left, right, dims, preferred_element_type=f32)


def halves(value):
    high = value.astype(bf16)
    return high, (value - high.astype(f32)).astype(bf16)


def window_rows(block):
    pieces = [block[u, 8 * w : 8 * w + 8, :] for w in range(4) for u in range(8)]
    return jnp.concatenate(pieces, axis=0)


def upstream_kernel(scale, cot_ref, wp3_ref, uhi_ref, ulo_ref, dohi_ref, dolo_ref, dotok_ref):
    upstream = window_rows(cot_ref) * scale
    uhi, ulo = halves(upstream)
    uhi_ref[...] = uhi
    ulo_ref[...] = ulo
    u3 = jnp.concatenate([uhi, uhi, ulo], axis=1)
    for at in range(0, 512, 128):
        hi, lo = halves(dot(wp3_ref[at : at + 128, :], u3, NT))
        dohi_ref[at : at + 128, :], dolo_ref[at : at + 128, :] = hi, lo
        dotok_ref[:, 2 * at : 2 * at + 128] = hi.T
        dotok_ref[:, 2 * at + 128 : 2 * at + 256] = lo.T


def swap(value):
    return jnp.concatenate([value[:, 64:], value[:, :64]], axis=1)


def block_diagonal(value, left, right):
    other = swap(value)
    zeros = jnp.zeros((32, 128), bf16)
    for even, odd in ((value, other), (other, value)):
        first = jnp.concatenate([even[0:32] * left, odd[32:64] * right, zeros, zeros], axis=0)
        second = jnp.concatenate([zeros, zeros, even[64:96] * left, odd[96:128] * right], axis=0)
        yield jnp.concatenate([first, second], axis=1)


def gather_diagonal(lane, pair_a, pair_b):
    low = lane < 64
    return jnp.concatenate(
        [
            jnp.where(low, pair_a[:32], swap(pair_b[:32])),
            jnp.where(low, swap(pair_a[32:]), pair_b[32:]),
        ],
        axis=0,
    )


def heads_product(left2, hi, lo, window):
    zeros = jnp.zeros((64, 256), bf16)
    right = jnp.concatenate([hi, lo, hi, zeros] if window == 0 else [hi, lo, zeros, hi], axis=0)
    product = dot(left2, right)
    return [product[:64, :128], product[64:, 128:]]


def fill(source, step, slot, wcat, xt_all):
    pkhi, pklo, kt, vt, rstd_tok, rstd_lane, qt = slot
    here = pl.ds(pl.multiple_of(step * 256, 256), 256)
    kept = {}

    def project(first):
        for at in range(first, first + 512, 128):
            rows = slice(at, at + 128)
            pkhi[rows, :], pklo[rows, :] = halves(dot(wcat[rows, :], kept["twice"]) * kept["rstd"])

    def turned(base, tok):
        for g in range(4):
            rows = slice(base + 128 * g, base + 128 * g + 128)
            high = pkhi[rows, :].T
            tok[g, :, 0:128] = high
            tok[g, :, 128:256] = pklo[rows, :].T
            if base:
                tok[g, :, 256:384] = high

    def begin():
        tile, side, x_all = source
        rows = [tile[step * 8 + 4 + u].astype(f32) for u in range(8)]
        ends = [side[step * 8 + 4 + u].astype(f32) for u in range(8)]
        pieces = []
        for w in range(4):
            for u in range(8):
                if w < 3:
                    pieces.append(rows[u][8 * w + 4 : 8 * w + 12])
                else:
                    pieces.append(jnp.concatenate([rows[u][28:], ends[u]], axis=0))
        tokens16 = jnp.concatenate(pieces, axis=0).astype(bf16)
        x_all[here, :] = tokens16
        xt = tokens16.T.astype(f32)
        xt16 = xt.astype(bf16)
        xt_all[:, here] = xt16
        mean = jnp.sum(xt, axis=0, keepdims=True) * (1.0 / 512)
        centered = xt - mean
        spread = jnp.sum(centered * centered, axis=0, keepdims=True) * (1.0 / 512)
        rstd = lax.rsqrt(spread + 1e-05)
        rstd_lane[...] = rstd * jnp.ones((8, 1), f32)
        rstd_tok[...] = jnp.transpose(jnp.broadcast_to(rstd, (128, 256)))
        kept["rstd"] = rstd
        kept["twice"] = jnp.concatenate([xt16, xt16], axis=0)

    def queries():
        project(0)
        turned(0, qt)

    def keys():
        project(512)
        turned(512, kt)

    def values():
        project(1024)
        turned(1024, vt)

    return [begin, queries, keys, values]


def main_kernel(
    flag_ref, tile_hbm, down_hbm, right_hbm, corner_hbm, wcat_hbm, bias_hbm, uhi_hbm, ulo_hbm, dohi_ref, dolo_ref, dotok_ref,
    own_hbm, other_hbm, ahi_ref, alo_ref, x_hbm,
    pkhi0, pklo0, kt0, vt0, rt0, rl0, qt0, pkhi1, pklo1, kt1, vt1, rt1, rl1, qt1,
    xt_all, ahi_all, alo_all, g_all, rel_acc,
    wcat, bias_ref, uhi_ref, ulo_ref, own_ref, other_ref, tile, side, x_all, in_sem, out_sem,
):
    step = pl.program_id(0)
    slots = ((pkhi0, pklo0, kt0, vt0, rt0, rl0, qt0), (pkhi1, pklo1, kt1, vt1, rt1, rl1, qt1))
    loads = [
        pltpu.make_async_copy(source, target, in_sem.at[n])
        for n, (source, target) in enumerate(
            (
                (tile_hbm, tile.at[:32]),
                (down_hbm, tile.at[32:]),
                (right_hbm, side.at[:32]),
                (corner_hbm, side.at[32:]),
                (wcat_hbm, wcat),
                (bias_hbm, bias_ref),
                (uhi_hbm, uhi_ref),
                (ulo_hbm, ulo_ref),
            )
        )
    ]
    source = (tile, side, x_all)
    lane = lax.broadcasted_iota(jnp.int32, (1, 128), 1)
    left16 = (lane < 64).astype(f32).astype(bf16)
    right16 = (lane >= 64).astype(f32).astype(bf16)
    lane2 = lax.broadcasted_iota(jnp.int32, (1, 256), 1) & 127
    head_of = [((lane2 >= 32 * j) & (lane2 < 32 * j + 32)).astype(f32).astype(bf16) for j in range(4)]
    row_of = lax.broadcasted_iota(jnp.int32, (64, 256), 0)
    lane_of = lax.broadcasted_iota(jnp.int32, (64, 256), 1)
    root = 1.0 / math.sqrt(32.0)

    def operands(g, slot):
        pkhi, pklo, kt, vt = slot[:4]
        rows_q, rows_k, rows_v = (slice(128 * g + base, 128 * g + base + 128) for base in (0, 512, 1024))
        unit = []
        for p in range(2):
            lanes = slice(128 * p, 128 * p + 128)
            qhi = list(block_diagonal(pkhi[rows_q, lanes], left16, right16))
            qlo = list(block_diagonal(pklo[rows_q, lanes], left16, right16))
            ohi = list(block_diagonal(dohi_ref[rows_q, lanes], left16, right16))
            olo = list(block_diagonal(dolo_ref[rows_q, lanes], left16, right16))
            both = []
            for rows in (rows_k, rows_v):
                high, low = pkhi[rows, lanes], pklo[rows, lanes]
                other = swap(high)
                one = high * left16 + other * right16
                two = other * left16 + high * right16
                both.append([jnp.concatenate([one, low], axis=1), jnp.concatenate([two, low], axis=1)])
            for w in range(2):
                unit.append((qhi[w], qlo[w], ohi[w], olo[w], both[0][w], both[1][w]))
        scores, products = [], []
        for n, (qh, ql, oh, ol, _, _) in enumerate(unit):
            at = 64 * n
            scores.append(dot(kt[g, at : at + 64, :], jnp.concatenate([qh, qh, ql], axis=0)))
            products.append(dot(vt[g, at : at + 64, :], jnp.concatenate([oh, oh, ol], axis=0)))
        return unit, scores, products

    def finish(g, state, slot, edge):
        unit, scores, products = state
        rstd_tok, rstd_lane, qt = slot[4:]
        rows_q = slice(128 * g, 128 * g + 128)
        cols_k = slice(128 * g + 512, 128 * g + 640)
        cols_v = slice(128 * g + 1024, 128 * g + 1152)
        probs, attended, dss, grad_q = [], [], [], []
        for n in range(4):
            s = scores[n] + bias_ref[g]
            if edge is not None:
                s = jnp.where(edge, -1000000000.0, s)
            e = jnp.exp(s - jnp.max(s, axis=0, keepdims=True))
            weights = e * (1.0 / jnp.sum(e, axis=0, keepdims=True))
            inner = jnp.sum(weights * products[n], axis=0, keepdims=True)
            probs.append(halves(weights))
            dss.append(weights * (products[n] - inner))
        rel_acc[g] = rel_acc[g] + ((dss[0] + dss[1]) + (dss[2] + dss[3]))
        dss = [halves(ds) for ds in dss]
        for n in range(4):
            attended.append(heads_product(unit[n][5], *probs[n], n % 2))
        for n in range(4):
            grad_q.append(heads_product(unit[n][4], *dss[n], n % 2))
        for pairs, tok, cols in ((probs, None, cols_v), (dss, qt, cols_k)):
            for n in range(4):
                at = 64 * n
                if tok is None:
                    both = dotok_ref[at : at + 64, 256 * g : 256 * g + 256]
                else:
                    both = tok[g, at : at + 64, :]
                to = pl.ds(pl.multiple_of(step * 256 + at, 64), 64)
                to_lo = pl.ds(pl.multiple_of(step * 256 + at + 1024, 64), 64)
                product = dot(
                    jnp.concatenate(pairs[n], axis=0),
                    jnp.concatenate([both * mask for mask in head_of], axis=0),
                )
                total = product[:64, :128] + product[64:, :128] + product[:64, 128:]
                g_all[to, cols], g_all[to_lo, cols] = halves(total * rstd_tok[at : at + 64, :])
        for p in range(2):
            lanes = slice(128 * p, 128 * p + 128)
            here_p = pl.ds(pl.multiple_of(step * 256 + 128 * p, 128), 128)
            here_p_lo = pl.ds(pl.multiple_of(step * 256 + 128 * p + 1024, 128), 128)
            one, two = 2 * p, 2 * p + 1
            att = jnp.concatenate([gather_diagonal(lane, attended[one][t], attended[two][t]) for t in range(2)], axis=0)
            att_hi, att_lo = halves(att)
            ahi_all[rows_q, here_p], alo_all[rows_q, here_p] = att_hi, att_lo
            ahi_ref[rows_q, lanes], alo_ref[rows_q, lanes] = att_hi, att_lo
            gq = jnp.concatenate([gather_diagonal(lane, grad_q[one][t], grad_q[two][t]) for t in range(2)], axis=0)
            gq = gq * (rstd_lane[0:1, lanes] * root)
            gq_hi, gq_lo = halves(gq)
            g_all[here_p, rows_q], g_all[here_p_lo, rows_q] = gq_hi.T, gq_lo.T

    def attention(slot, beside, edge):
        state = operands(0, slot)
        for g in range(4):
            if beside is not None:
                beside[g]()
            after = operands(g + 1, slot) if g < 3 else None
            finish(g, state, slot, edge)
            state = after

    @pl.when(step == 0)
    def _():
        for load in loads:
            load.start()
        rel_acc[...] = jnp.zeros_like(rel_acc)
        parts = fill(source, 0, slots[0], wcat, xt_all)
        for load in loads[:4]:
            load.wait()
        parts[0]()
        loads[4].wait()
        for part in parts[1:]:
            part()
        loads[5].wait()

    @pl.when(step % 2 == 0)
    def _():
        attention(slots[0], fill(source, step + 1, slots[1], wcat, xt_all), None)

    @pl.when(step == 1)
    def _():
        attention(slots[1], fill(source, step + 1, slots[0], wcat, xt_all), None)

    @pl.when(step == 3)
    def _():
        keep = pltpu.make_async_copy(x_all, x_hbm, in_sem.at[8])
        keep.start()
        crossing = ((row_of >= 32) != ((lane_of & 63) >= 32)) & (flag_ref[0] > 0)
        attention(slots[1], None, crossing)
        loads[6].wait()
        loads[7].wait()
        sub = lax.broadcasted_iota(jnp.int32, (1, 8, 128), 1)
        first = flag_ref[1] == 0
        stores = [keep]

        def send(k):
            for n, (source, target) in enumerate(((own_ref, own_hbm), (other_ref, other_hbm))):
                copy = pltpu.make_async_copy(
                    source.at[k], target.at[k], out_sem.at[n, k]
                )
                copy.start()
                stores.append(copy)

        def pack(k, value):
            a, b = value[:, :128].reshape(64, 8, 128), value[:, 128:].reshape(64, 8, 128)
            aa = jnp.concatenate([a[:, 4:], a[:, :4]], axis=1)
            bb = jnp.concatenate([b[:, 4:], b[:, :4]], axis=1)
            even = jnp.where(sub < 4, a, bb).reshape(4, 2, 8, 8, 128)
            odd = jnp.where(sub < 4, aa, b).reshape(4, 2, 8, 8, 128)
            for n, block in ((0, even), (1, odd)):
                own_ref[k, :, :, n] = jnp.where(first, block[:, 0], block[:, 1])
                other_ref[k, :, :, n] = jnp.where(first, block[:, 1], block[:, 0])
            send(k)

        twice = jnp.concatenate([xt_all[...], xt_all[...]], axis=1)
        for k in range(6):
            value = dot(twice, g_all[:, 256 * k : 256 * k + 256])
            pack(k, value - jnp.sum(value, axis=0, keepdims=True) * (1.0 / 512))
        for k in range(2):
            cols = slice(256 * k, 256 * k + 256)
            u = uhi_ref[:, cols]
            value = (
                dot(ahi_all[...], u) + dot(alo_all[...], u) + dot(ahi_all[...], ulo_ref[:, cols])
            )
            pack(6 + k, value)
        for g in range(4):
            turned = jnp.transpose(
                jnp.concatenate([rel_acc[g], jnp.zeros((64, 256), f32)], axis=0)
            ).reshape(2, 8, 2, 8, 128)
            own_ref[8, g] = jnp.where(first, turned[0], turned[1])
            other_ref[8, g] = jnp.where(first, turned[1], turned[0])
        send(8)
        for store in stores:
            store.wait()


def output_kernel(x_ref, ahi_ref, alo_ref, wp3_ref, out_ref):
    tokens = x_ref[...].astype(f32)
    tok_hi, tok_lo = ahi_ref[...].T, alo_ref[...].T
    result = tokens + dot(jnp.concatenate([tok_hi, tok_lo, tok_hi], axis=1), wp3_ref[...])
    for w in range(4):
        for u in range(8):
            out_ref[u, 8 * w : 8 * w + 8, :] = result[64 * w + 8 * u : 64 * w + 8 * u + 8, :]


def full(shape):
    return pl.BlockSpec(shape, lambda a: (0,) * len(shape))


def once(shape):
    return pl.BlockSpec(shape, lambda a: (0,) * len(shape), pipeline_mode=pl.Buffered(1))


def upstream_call(cot, wp3, scale):
    return pl.pallas_call(
        functools.partial(upstream_kernel, scale),
        grid=(4,),
        in_specs=[pl.BlockSpec((8, 32, 512), lambda a: (a, 0, 0)), full((512, 1536))],
        out_specs=[
            pl.BlockSpec((256, 512), lambda a: (a, 0)),
            pl.BlockSpec((256, 512), lambda a: (a, 0)),
            pl.BlockSpec((512, 256), lambda a: (0, a)),
            pl.BlockSpec((512, 256), lambda a: (0, a)),
            pl.BlockSpec((256, 1024), lambda a: (a, 0)),
        ],
        out_shape=[jax.ShapeDtypeStruct((1024, 512), bf16)] * 2
        + [jax.ShapeDtypeStruct((512, 1024), bf16)] * 2
        + [jax.ShapeDtypeStruct((1024, 1024), bf16)],
        compiler_params=pltpu.CompilerParams(vmem_limit_bytes=24 << 20),
        cost_estimate=pl.CostEstimate(flops=1600000000, bytes_accessed=8 << 20, transcendentals=0),
        name="upstream",
    )(cot, wp3)


def main_call(flags, tile, down, right, corner, wcat, bias, uhi, ulo, dohi, dolo, dotok):
    anywhere = pl.BlockSpec(memory_space=pl.ANY)
    column = pl.BlockSpec((512, 256), lambda a: (0, a))
    slot = [
        pltpu.VMEM((1536, 256), bf16),
        pltpu.VMEM((1536, 256), bf16),
        pltpu.VMEM((4, 256, 384), bf16),
        pltpu.VMEM((4, 256, 384), bf16),
        pltpu.VMEM((256, 128), f32),
        pltpu.VMEM((8, 256), f32),
        pltpu.VMEM((4, 256, 256), bf16),
    ]
    terms = (9, 4, 8, 2, 8, 128)
    return pl.pallas_call(
        main_kernel,
        grid=(4,),
        in_specs=[pl.BlockSpec(memory_space=pltpu.SMEM)]
        + [anywhere] * 8
        + [column] * 2
        + [pl.BlockSpec((256, 1024), lambda a: (a, 0))],
        out_specs=[anywhere] * 2 + [column] * 2 + [anywhere],
        out_shape=[jax.ShapeDtypeStruct(terms, f32)] * 2
        + [jax.ShapeDtypeStruct((512, 1024), bf16)] * 2
        + [jax.ShapeDtypeStruct((1024, 512), bf16)],
        scratch_shapes=slot
        + slot
        + [
            pltpu.VMEM((512, 1024), bf16),
            pltpu.VMEM((512, 1024), bf16),
            pltpu.VMEM((512, 1024), bf16),
            pltpu.VMEM((2048, 1536), bf16),
            pltpu.VMEM((4, 64, 256), f32),
            pltpu.VMEM((1536, 1024), bf16),
            pltpu.VMEM((4, 64, 256), f32),
            pltpu.VMEM((1024, 512), bf16),
            pltpu.VMEM((1024, 512), bf16),
            pltpu.VMEM(terms, f32),
            pltpu.VMEM(terms, f32),
            pltpu.VMEM((36, 32, 512), bf16),
            pltpu.VMEM((36, 4, 512), bf16),
            pltpu.VMEM((1024, 512), bf16),
            pltpu.SemaphoreType.DMA((9,)),
            pltpu.SemaphoreType.DMA((2, 9)),
        ],
        compiler_params=pltpu.CompilerParams(vmem_limit_bytes=56 << 20),
        cost_estimate=pl.CostEstimate(flops=16000000000, bytes_accessed=24 << 20, transcendentals=1 << 20),
        name="block",
    )(flags, tile, down, right, corner, wcat, bias, uhi, ulo, dohi, dolo, dotok)


def output_call(x, ahi, alo, wp3):
    column = pl.BlockSpec((512, 256), lambda a: (0, a))
    return pl.pallas_call(
        output_kernel,
        grid=(4,),
        in_specs=[pl.BlockSpec((256, 512), lambda a: (a, 0)), column, column, once((1536, 512))],
        out_specs=pl.BlockSpec((8, 32, 512), lambda a: (a, 0, 0)),
        out_shape=jax.ShapeDtypeStruct((32, 32, 512), f32),
        compiler_params=pltpu.CompilerParams(vmem_limit_bytes=20 << 20),
        cost_estimate=pl.CostEstimate(flops=1600000000, bytes_accessed=8 << 20, transcendentals=0),
        name="output",
    )(x, ahi, alo, wp3)


def split(w):
    high = lax.reduce_precision(w, 8, 7)
    return high.astype(bf16), (w - high).astype(bf16)


def weights(gain, w_qkv, w_proj, rel_bias):
    root = 1.0 / math.sqrt(32.0)
    width = w_proj.shape[0]
    wc = gain[:, None] * w_qkv
    wc = wc * jnp.where(jnp.arange(3 * width) < width, root, 1.0)[None, :]
    wc = (wc - jnp.mean(wc, axis=0, keepdims=True)).T
    wcat = jnp.concatenate(split(wc), axis=1)
    phi, plo = split(w_proj)
    wp_rows = jnp.concatenate([phi, phi, plo], axis=0)
    wp_cols = jnp.concatenate([phi, plo, phi], axis=1)
    bias = rel_bias.reshape(4, 4, 64, 64).transpose(0, 3, 1, 2).reshape(4, 64, 256)
    return wcat, wp_rows, wp_cols, bias


ORDER = (0, 2, 1, 3)


def band_kernel(a_ref, b_ref, c_ref, d_ref, gain_ref, rows_ref, qkv_ref, proj_ref, gain_out, rel_ref):
    total = (a_ref[...] + b_ref[...]) + (c_ref[...] + d_ref[...])
    gain = gain_ref[...]
    sums = jnp.zeros((4, 128), f32)
    for k in range(12):
        part = total[4 * k : 4 * k + 4]
        cols = slice(128 * k, 128 * k + 128)
        qkv_ref[:, cols] = part * gain
        sums = sums + part * rows_ref[:, cols]
    for k in range(4):
        proj_ref[:, 128 * k : 128 * k + 128] = total[48 + 4 * k : 52 + 4 * k]
    rel_ref[...] = total[64:, :64]
    column = jnp.sum(sums, axis=1, keepdims=True)
    for n in range(4):
        gain_out[n] = column[n, 0]


def band_call(parts, gain, rows):
    return pl.pallas_call(
        band_kernel,
        out_shape=[
            jax.ShapeDtypeStruct((4, 1536), f32),
            jax.ShapeDtypeStruct((4, 512), f32),
            jax.ShapeDtypeStruct((4,), f32),
            jax.ShapeDtypeStruct((8, 64), f32),
        ],
        out_specs=[pl.BlockSpec(memory_space=pltpu.VMEM)] * 2
        + [pl.BlockSpec(memory_space=pltpu.SMEM), pl.BlockSpec(memory_space=pltpu.VMEM)],
        name="band",
    )(*parts, gain, rows)


def turn(size, by):
    return [(i, (i + by) % size) for i in range(size)]


def fetch(slots, plan_rank, plan_slot, early):
    count = lax.axis_size("buf")
    slot_count, tile_tokens, width = slots.shape[3:]
    part = tile_tokens // count
    spread = slots.reshape(slot_count, count, part, width).transpose(1, 0, 2, 3)
    held = lax.all_to_all(spread, "buf", split_axis=0, concat_axis=0, tiled=True)
    held, early = lax.optimization_barrier((held, early))
    held = held.reshape(count * slot_count, part, width)
    wanted = plan_rank.reshape(count) * slot_count + plan_slot.reshape(count)
    asked = held.at[wanted].get(mode="promise_in_bounds")
    tile = lax.all_to_all(asked, "buf", split_axis=0, concat_axis=0, tiled=True)
    return tile.reshape(32, 32, width), early


def edge_kernel(top_ref, side_ref, down_ref, right_ref, corner_ref):
    half = WSIDE // 2
    down_ref[...] = top_ref[...]
    right_ref[...] = side_ref[:, :half, :]
    corner_ref[...] = top_ref[:, :half, :]


def edge_call(tile):
    half, rows, width = WSIDE // 2, tile.shape[0], tile.shape[-1]
    return pl.pallas_call(
        edge_kernel,
        grid=(1,),
        in_specs=[
            pl.BlockSpec((half, rows, width), lambda a: (0, 0, 0)),
            pl.BlockSpec((rows, 16, width), lambda a: (0, 0, 0)),
        ],
        out_specs=[full((half, rows, width)), full((rows, half, width)), full((half, half, width))],
        out_shape=[
            jax.ShapeDtypeStruct(shape, bf16)
            for shape in ((half, rows, width), (rows, half, width), (half, half, width))
        ],
        compiler_params=pltpu.CompilerParams(vmem_limit_bytes=56 << 20),
        name="edges",
    )(tile, tile)


def halo(tile):
    lat, lon = lax.axis_size("lat"), lax.axis_size("lon")
    down, right, corner = edge_call(tile)
    down = lax.ppermute(down, "lat", turn(lat, -1))
    right = lax.ppermute(right, "lon", turn(lon, -1))
    corner_pairs = [
        (i * lon + j, (i - 1) % lat * lon + (j - 1) % lon) for i in range(lat) for j in range(lon)
    ]
    corner = lax.ppermute(corner, ("lat", "lon"), corner_pairs)
    return tile, down, right, corner


def send(blocks, axis, size, step):
    moved = [lax.ppermute(b, axis, turn(size, step * by)) for b, by in zip(blocks[1:], ORDER[1:])]
    return [blocks[0], *moved]


def choose(blocks, dim, me):
    return [lax.dynamic_index_in_dim(blocks, (me + by) % 4, dim, keepdims=False) for by in ORDER]


def total(parts):
    return (parts[0] + parts[1]) + (parts[2] + parts[3])


def sum_bands(own, other, work):
    buf, lat, lon = lax.axis_index("buf"), lax.axis_index("lat"), lax.axis_index("lon")
    got = lax.ppermute(other, "buf", [(i, i ^ 1) for i in range(8)])
    got, output = lax.optimization_barrier((got, work()))
    x = (own + got).reshape(9, 4, 4, 4, 8, 128)
    left = total(send(choose(x[:5], 3, lon), "lon", 4, 1))
    right = total(send(choose(x[5:], 2, lat), "lat", 4, 1))
    left = total(send(choose(left, 2, lat), "lat", 4, 1))
    right = total(send(choose(right, 2, lon), "lon", 4, 1))
    x = jnp.concatenate([left, right], axis=0)
    return output, [part.reshape(72, 128) for part in send(choose(x, 1, buf // 2), "buf", 8, 2)]


def on_device(slots, plan_rank, plan_slot, gain, w_qkv, w_proj, rel_bias, cotangent):
    width = gain.shape[0]
    wcat, wp_rows, wp_cols, bias = weights(gain, w_qkv, w_proj, rel_bias)
    tokens = 128 * cotangent.shape[1] * cotangent.shape[2] * cotangent.shape[3]
    ready = upstream_call(cotangent[0, 0], wp_cols, 1.0 / math.sqrt(tokens))
    place = (lax.axis_index("buf") * 4 + lax.axis_index("lat")) * 4 + lax.axis_index("lon")
    my_gain = jnp.broadcast_to(lax.dynamic_slice_in_dim(gain, place * 4, 4)[:, None], (4, 128))
    my_rows = lax.dynamic_slice_in_dim(w_qkv, place * 4, 4)
    last = lax.axis_index("lat") == lax.axis_size("lat") - 1
    flags = jnp.stack([last.astype(jnp.int32), lax.axis_index("buf") % 2])
    early = (ready, bias, wp_rows, wcat, my_gain, my_rows, flags)
    tile, early = fetch(slots, plan_rank, plan_slot, early)
    ready, bias, wp_rows, wcat, my_gain, my_rows, flags = early
    own, other, ahi, alo, x = main_call(flags, *halo(tile), wcat, bias, *ready)
    output, parts = sum_bands(own, other, lambda: output_call(x, ahi, alo, wp_rows))
    grad_qkv, grad_proj, grad_gain, grad_rel = band_call(parts, my_gain, my_rows)
    return (output.reshape(cotangent.shape), grad_qkv, grad_proj, grad_gain, grad_rel)


def solution(mesh):
    placed = (
        P("buf", "lat", "lon", None, None, None),
        P("lat", "lon", None, None),
        P("lat", "lon", None),
        P(),
        P(),
        P(),
        P(),
        P("buf", None, "lat", "lon", None),
    )
    return jax.shard_map(
        on_device,
        mesh=mesh,
        in_specs=placed,
        out_specs=(
            P("buf", None, "lat", "lon", None),
            P(("buf", "lat", "lon"), None),
            P(("buf", "lat", "lon"), None),
            P(("buf", "lat", "lon")),
            P(("buf", "lat", "lon"), None),
        ),
        check_vma=False,
    )
```

```python
import functools
import math

import jax
import jax.numpy as jnp
from jax import lax
from jax.experimental import pallas as pl
from jax.experimental.pallas import tpu as pltpu
from jax.sharding import PartitionSpec as P

HEADS = 16
WSIDE = 8
NT = (((1,), (1,)), ((), ()))
NN = (((1,), (0,)), ((), ()))
f32, bf16 = jnp.float32, jnp.bfloat16


def dot(left, right, dims=NN):
    return lax.dot_general(left, right, dims, preferred_element_type=f32)


def halves(value):
    high = value.astype(bf16)
    return high, (value - high.astype(f32)).astype(bf16)


def window_rows(block):
    pieces = [block[u, 8 * w : 8 * w + 8, :] for w in range(4) for u in range(8)]
    return jnp.concatenate(pieces, axis=0)


def upstream_kernel(scale, cot_ref, phi_ref, plo_ref, uhi_ref, ulo_ref, dohi_ref, dolo_ref, dotok_ref):
    upstream = window_rows(cot_ref) * scale
    uhi, ulo = halves(upstream)
    uhi_ref[...] = uhi
    ulo_ref[...] = ulo
    u3 = jnp.concatenate([uhi, uhi, ulo], axis=1)
    for at in range(0, 512, 128):
        phi = phi_ref[at : at + 128, :]
        rows = jnp.concatenate([phi, plo_ref[at : at + 128, :], phi], axis=1)
        hi, lo = halves(dot(rows, u3, NT))
        dohi_ref[at : at + 128, :], dolo_ref[at : at + 128, :] = hi, lo
        dotok_ref[:, 2 * at : 2 * at + 128] = hi.T
        dotok_ref[:, 2 * at + 128 : 2 * at + 256] = lo.T


def swap(value):
    return jnp.concatenate([value[:, 64:], value[:, :64]], axis=1)


def block_diagonal(value, left, right):
    other = swap(value)
    zeros = jnp.zeros((32, 128), bf16)
    for even, odd in ((value, other), (other, value)):
        first = jnp.concatenate([even[0:32] * left, odd[32:64] * right, zeros, zeros], axis=0)
        second = jnp.concatenate([zeros, zeros, even[64:96] * left, odd[96:128] * right], axis=0)
        yield jnp.concatenate([first, second], axis=1)


def gather_diagonal(lane, pair_a, pair_b):
    low = lane < 64
    return jnp.concatenate(
        [
            jnp.where(low, pair_a[:32], swap(pair_b[:32])),
            jnp.where(low, swap(pair_a[32:]), pair_b[32:]),
        ],
        axis=0,
    )


def heads_product(left2, hi, lo, window):
    zeros = jnp.zeros((64, 256), bf16)
    right = jnp.concatenate([hi, lo, hi, zeros] if window == 0 else [hi, lo, zeros, hi], axis=0)
    product = dot(left2, right)
    return [product[:64, :128], product[64:, 128:]]


def fill(source, step, slot, wcat, xt_all):
    pkhi, pklo, kt, vt, rstd_tok, rstd_lane, qt = slot
    here = pl.ds(pl.multiple_of(step * 256, 256), 256)
    kept = {}

    def project(first):
        for at in range(first, first + 512, 128):
            rows = slice(at, at + 128)
            pkhi[rows, :], pklo[rows, :] = halves(dot(wcat[rows, :], kept["twice"]) * kept["rstd"])

    def turned(base, tok):
        for g in range(4):
            rows = slice(base + 128 * g, base + 128 * g + 128)
            high = pkhi[rows, :].T
            tok[g, :, 0:128] = high
            tok[g, :, 128:256] = pklo[rows, :].T
            if base:
                tok[g, :, 256:384] = high

    def begin():
        tile, side, x_all = source
        rows = [tile[step * 8 + 4 + u].astype(f32) for u in range(8)]
        ends = [side[step * 8 + 4 + u].astype(f32) for u in range(8)]
        pieces = []
        for w in range(4):
            for u in range(8):
                if w < 3:
                    pieces.append(rows[u][8 * w + 4 : 8 * w + 12])
                else:
                    pieces.append(jnp.concatenate([rows[u][28:], ends[u]], axis=0))
        tokens16 = jnp.concatenate(pieces, axis=0).astype(bf16)
        x_all[here, :] = tokens16
        xt = tokens16.T.astype(f32)
        xt16 = xt.astype(bf16)
        xt_all[:, here] = xt16
        mean = jnp.sum(xt, axis=0, keepdims=True) * (1.0 / 512)
        centered = xt - mean
        spread = jnp.sum(centered * centered, axis=0, keepdims=True) * (1.0 / 512)
        rstd = lax.rsqrt(spread + 1e-05)
        rstd_lane[...] = rstd * jnp.ones((8, 1), f32)
        rstd_tok[...] = jnp.transpose(jnp.broadcast_to(rstd, (128, 256)))
        kept["rstd"] = rstd
        kept["twice"] = jnp.concatenate([xt16, xt16], axis=0)

    def queries():
        project(0)
        turned(0, qt)

    def keys():
        project(512)
        turned(512, kt)

    def values():
        project(1024)
        turned(1024, vt)

    return [begin, queries, keys, values]


def main_kernel(
    flag_ref, tile_hbm, down_hbm, right_hbm, corner_hbm, chi_hbm, clo_hbm, bias_hbm, uhi_hbm, ulo_hbm, dohi_ref, dolo_ref, dotok_ref,
    own_hbm, other_hbm, ahi_ref, alo_ref, x_hbm,
    pkhi0, pklo0, kt0, vt0, rt0, rl0, qt0, pkhi1, pklo1, kt1, vt1, rt1, rl1, qt1,
    xt_all, ahi_all, alo_all, g_all, rel_acc,
    wcat, bias_ref, uhi_ref, ulo_ref, own_ref, other_ref, tile, side, x_all, in_sem, out_sem,
):
    step = pl.program_id(0)
    slots = ((pkhi0, pklo0, kt0, vt0, rt0, rl0, qt0), (pkhi1, pklo1, kt1, vt1, rt1, rl1, qt1))
    loads = [
        pltpu.make_async_copy(source, target, in_sem.at[n])
        for n, (source, target) in enumerate(
            (
                (tile_hbm, tile.at[:32]),
                (down_hbm, tile.at[32:]),
                (right_hbm, side.at[:32]),
                (corner_hbm, side.at[32:]),
                (chi_hbm, wcat.at[:, :512]),
                (clo_hbm, wcat.at[:, 512:]),
                (bias_hbm, bias_ref),
                (uhi_hbm, uhi_ref),
                (ulo_hbm, ulo_ref),
            )
        )
    ]
    source = (tile, side, x_all)
    lane = lax.broadcasted_iota(jnp.int32, (1, 128), 1)
    left16 = (lane < 64).astype(f32).astype(bf16)
    right16 = (lane >= 64).astype(f32).astype(bf16)
    lane2 = lax.broadcasted_iota(jnp.int32, (1, 256), 1) & 127
    head_of = [((lane2 >= 32 * j) & (lane2 < 32 * j + 32)).astype(f32).astype(bf16) for j in range(4)]
    row_of = lax.broadcasted_iota(jnp.int32, (64, 256), 0)
    lane_of = lax.broadcasted_iota(jnp.int32, (64, 256), 1)
    root = 1.0 / math.sqrt(32.0)

    def operands(g, slot):
        pkhi, pklo, kt, vt = slot[:4]
        rows_q, rows_k, rows_v = (slice(128 * g + base, 128 * g + base + 128) for base in (0, 512, 1024))
        unit = []
        for p in range(2):
            lanes = slice(128 * p, 128 * p + 128)
            qhi = list(block_diagonal(pkhi[rows_q, lanes], left16, right16))
            qlo = list(block_diagonal(pklo[rows_q, lanes], left16, right16))
            ohi = list(block_diagonal(dohi_ref[rows_q, lanes], left16, right16))
            olo = list(block_diagonal(dolo_ref[rows_q, lanes], left16, right16))
            both = []
            for rows in (rows_k, rows_v):
                high, low = pkhi[rows, lanes], pklo[rows, lanes]
                other = swap(high)
                one = high * left16 + other * right16
                two = other * left16 + high * right16
                both.append([jnp.concatenate([one, low], axis=1), jnp.concatenate([two, low], axis=1)])
            for w in range(2):
                unit.append((qhi[w], qlo[w], ohi[w], olo[w], both[0][w], both[1][w]))
        scores, products = [], []
        for n, (qh, ql, oh, ol, _, _) in enumerate(unit):
            at = 64 * n
            scores.append(dot(kt[g, at : at + 64, :], jnp.concatenate([qh, qh, ql], axis=0)))
            products.append(dot(vt[g, at : at + 64, :], jnp.concatenate([oh, oh, ol], axis=0)))
        return unit, scores, products

    def finish(g, state, slot, edge):
        unit, scores, products = state
        rstd_tok, rstd_lane, qt = slot[4:]
        rows_q = slice(128 * g, 128 * g + 128)
        cols_k = slice(128 * g + 512, 128 * g + 640)
        cols_v = slice(128 * g + 1024, 128 * g + 1152)
        probs, attended, dss, grad_q = [], [], [], []
        for n in range(4):
            s = scores[n] + bias_ref[g]
            if edge is not None:
                s = jnp.where(edge, -1000000000.0, s)
            e = jnp.exp(s - jnp.max(s, axis=0, keepdims=True))
            weights = e * (1.0 / jnp.sum(e, axis=0, keepdims=True))
            inner = jnp.sum(weights * products[n], axis=0, keepdims=True)
            probs.append(halves(weights))
            dss.append(weights * (products[n] - inner))
        rel_acc[g] = rel_acc[g] + ((dss[0] + dss[1]) + (dss[2] + dss[3]))
        dss = [halves(ds) for ds in dss]
        for n in range(4):
            attended.append(heads_product(unit[n][5], *probs[n], n % 2))
        for n in range(4):
            grad_q.append(heads_product(unit[n][4], *dss[n], n % 2))
        for pairs, tok, cols in ((probs, None, cols_v), (dss, qt, cols_k)):
            for n in range(4):
                at = 64 * n
                if tok is None:
                    both = dotok_ref[at : at + 64, 256 * g : 256 * g + 256]
                else:
                    both = tok[g, at : at + 64, :]
                to = pl.ds(pl.multiple_of(step * 256 + at, 64), 64)
                to_lo = pl.ds(pl.multiple_of(step * 256 + at + 1024, 64), 64)
                product = dot(
                    jnp.concatenate(pairs[n], axis=0),
                    jnp.concatenate([both * mask for mask in head_of], axis=0),
                )
                total = product[:64, :128] + product[64:, :128] + product[:64, 128:]
                g_all[to, cols], g_all[to_lo, cols] = halves(total * rstd_tok[at : at + 64, :])
        for p in range(2):
            lanes = slice(128 * p, 128 * p + 128)
            here_p = pl.ds(pl.multiple_of(step * 256 + 128 * p, 128), 128)
            here_p_lo = pl.ds(pl.multiple_of(step * 256 + 128 * p + 1024, 128), 128)
            one, two = 2 * p, 2 * p + 1
            att = jnp.concatenate([gather_diagonal(lane, attended[one][t], attended[two][t]) for t in range(2)], axis=0)
            att_hi, att_lo = halves(att)
            ahi_all[rows_q, here_p], alo_all[rows_q, here_p] = att_hi, att_lo
            ahi_ref[rows_q, lanes], alo_ref[rows_q, lanes] = att_hi, att_lo
            gq = jnp.concatenate([gather_diagonal(lane, grad_q[one][t], grad_q[two][t]) for t in range(2)], axis=0)
            gq = gq * (rstd_lane[0:1, lanes] * root)
            gq_hi, gq_lo = halves(gq)
            g_all[here_p, rows_q], g_all[here_p_lo, rows_q] = gq_hi.T, gq_lo.T

    def attention(slot, beside, edge):
        state = operands(0, slot)
        for g in range(4):
            if beside is not None:
                beside[g]()
            after = operands(g + 1, slot) if g < 3 else None
            finish(g, state, slot, edge)
            state = after

    @pl.when(step == 0)
    def _():
        for load in loads:
            load.start()
        rel_acc[...] = jnp.zeros_like(rel_acc)
        parts = fill(source, 0, slots[0], wcat, xt_all)
        for load in loads[:4]:
            load.wait()
        parts[0]()
        loads[4].wait()
        loads[5].wait()
        for part in parts[1:]:
            part()
        loads[6].wait()

    @pl.when(step % 2 == 0)
    def _():
        attention(slots[0], fill(source, step + 1, slots[1], wcat, xt_all), None)

    @pl.when(step == 1)
    def _():
        attention(slots[1], fill(source, step + 1, slots[0], wcat, xt_all), None)

    @pl.when(step == 3)
    def _():
        keep = pltpu.make_async_copy(x_all, x_hbm, in_sem.at[9])
        keep.start()
        crossing = ((row_of >= 32) != ((lane_of & 63) >= 32)) & (flag_ref[0] > 0)
        attention(slots[1], None, crossing)
        loads[7].wait()
        loads[8].wait()
        sub = lax.broadcasted_iota(jnp.int32, (1, 8, 128), 1)
        first = flag_ref[1] == 0
        stores = [keep]

        def send(k):
            for n, (source, target) in enumerate(((own_ref, own_hbm), (other_ref, other_hbm))):
                copy = pltpu.make_async_copy(
                    source.at[k], target.at[k], out_sem.at[n, k]
                )
                copy.start()
                stores.append(copy)

        def pack(k, value):
            a, b = value[:, :128].reshape(64, 8, 128), value[:, 128:].reshape(64, 8, 128)
            aa = jnp.concatenate([a[:, 4:], a[:, :4]], axis=1)
            bb = jnp.concatenate([b[:, 4:], b[:, :4]], axis=1)
            even = jnp.where(sub < 4, a, bb).reshape(4, 2, 8, 8, 128)
            odd = jnp.where(sub < 4, aa, b).reshape(4, 2, 8, 8, 128)
            for n, block in ((0, even), (1, odd)):
                own_ref[k, :, :, n] = jnp.where(first, block[:, 0], block[:, 1])
                other_ref[k, :, :, n] = jnp.where(first, block[:, 1], block[:, 0])
            send(k)

        twice = jnp.concatenate([xt_all[...], xt_all[...]], axis=1)
        for k in range(6):
            value = dot(twice, g_all[:, 256 * k : 256 * k + 256])
            pack(k, value - jnp.sum(value, axis=0, keepdims=True) * (1.0 / 512))
        for k in range(2):
            cols = slice(256 * k, 256 * k + 256)
            u = uhi_ref[:, cols]
            value = (
                dot(ahi_all[...], u) + dot(alo_all[...], u) + dot(ahi_all[...], ulo_ref[:, cols])
            )
            pack(6 + k, value)
        for g in range(4):
            turned = jnp.transpose(
                jnp.concatenate([rel_acc[g], jnp.zeros((64, 256), f32)], axis=0)
            ).reshape(2, 8, 2, 8, 128)
            own_ref[8, g] = jnp.where(first, turned[0], turned[1])
            other_ref[8, g] = jnp.where(first, turned[1], turned[0])
        send(8)
        for store in stores:
            store.wait()


def output_kernel(x_ref, ahi_ref, alo_ref, phi_ref, plo_ref, out_ref):
    tokens = x_ref[...].astype(f32)
    tok_hi, tok_lo = ahi_ref[...].T, alo_ref[...].T
    phi = phi_ref[...]
    wp3 = jnp.concatenate([phi, phi, plo_ref[...]], axis=0)
    result = tokens + dot(jnp.concatenate([tok_hi, tok_lo, tok_hi], axis=1), wp3)
    for w in range(4):
        for u in range(8):
            out_ref[u, 8 * w : 8 * w + 8, :] = result[64 * w + 8 * u : 64 * w + 8 * u + 8, :]


def full(shape):
    return pl.BlockSpec(shape, lambda a: (0,) * len(shape))


def once(shape):
    return pl.BlockSpec(shape, lambda a: (0,) * len(shape), pipeline_mode=pl.Buffered(1))


def upstream_call(cot, phi, plo, scale):
    return pl.pallas_call(
        functools.partial(upstream_kernel, scale),
        grid=(4,),
        in_specs=[pl.BlockSpec((8, 32, 512), lambda a: (a, 0, 0))] + [full((512, 512))] * 2,
        out_specs=[
            pl.BlockSpec((256, 512), lambda a: (a, 0)),
            pl.BlockSpec((256, 512), lambda a: (a, 0)),
            pl.BlockSpec((512, 256), lambda a: (0, a)),
            pl.BlockSpec((512, 256), lambda a: (0, a)),
            pl.BlockSpec((256, 1024), lambda a: (a, 0)),
        ],
        out_shape=[jax.ShapeDtypeStruct((1024, 512), bf16)] * 2
        + [jax.ShapeDtypeStruct((512, 1024), bf16)] * 2
        + [jax.ShapeDtypeStruct((1024, 1024), bf16)],
        compiler_params=pltpu.CompilerParams(vmem_limit_bytes=24 << 20),
        cost_estimate=pl.CostEstimate(flops=1600000000, bytes_accessed=8 << 20, transcendentals=0),
        name="upstream",
    )(cot, phi, plo)


def main_call(flags, tile, down, right, corner, chi, clo, bias, uhi, ulo, dohi, dolo, dotok):
    anywhere = pl.BlockSpec(memory_space=pl.ANY)
    column = pl.BlockSpec((512, 256), lambda a: (0, a))
    slot = [
        pltpu.VMEM((1536, 256), bf16),
        pltpu.VMEM((1536, 256), bf16),
        pltpu.VMEM((4, 256, 384), bf16),
        pltpu.VMEM((4, 256, 384), bf16),
        pltpu.VMEM((256, 128), f32),
        pltpu.VMEM((8, 256), f32),
        pltpu.VMEM((4, 256, 256), bf16),
    ]
    terms = (9, 4, 8, 2, 8, 128)
    return pl.pallas_call(
        main_kernel,
        grid=(4,),
        in_specs=[pl.BlockSpec(memory_space=pltpu.SMEM)]
        + [anywhere] * 9
        + [column] * 2
        + [pl.BlockSpec((256, 1024), lambda a: (a, 0))],
        out_specs=[anywhere] * 2 + [column] * 2 + [anywhere],
        out_shape=[jax.ShapeDtypeStruct(terms, f32)] * 2
        + [jax.ShapeDtypeStruct((512, 1024), bf16)] * 2
        + [jax.ShapeDtypeStruct((1024, 512), bf16)],
        scratch_shapes=slot
        + slot
        + [
            pltpu.VMEM((512, 1024), bf16),
            pltpu.VMEM((512, 1024), bf16),
            pltpu.VMEM((512, 1024), bf16),
            pltpu.VMEM((2048, 1536), bf16),
            pltpu.VMEM((4, 64, 256), f32),
            pltpu.VMEM((1536, 1024), bf16),
            pltpu.VMEM((4, 64, 256), f32),
            pltpu.VMEM((1024, 512), bf16),
            pltpu.VMEM((1024, 512), bf16),
            pltpu.VMEM(terms, f32),
            pltpu.VMEM(terms, f32),
            pltpu.VMEM((36, 32, 512), bf16),
            pltpu.VMEM((36, 4, 512), bf16),
            pltpu.VMEM((1024, 512), bf16),
            pltpu.SemaphoreType.DMA((10,)),
            pltpu.SemaphoreType.DMA((2, 9)),
        ],
        compiler_params=pltpu.CompilerParams(vmem_limit_bytes=56 << 20),
        cost_estimate=pl.CostEstimate(flops=16000000000, bytes_accessed=24 << 20, transcendentals=1 << 20),
        name="block",
    )(flags, tile, down, right, corner, chi, clo, bias, uhi, ulo, dohi, dolo, dotok)


def output_call(half, before, x, ahi, alo, phi, plo):
    body, first, given, alias = output_kernel, [], [], {}
    if before is not None:
        first, given, alias = [pl.BlockSpec(memory_space=pl.ANY)], [before], {0: 0}

        def body(_, *refs):
            output_kernel(*refs)

    column = pl.BlockSpec((512, 256), lambda a: (0, a + 2 * half))
    return pl.pallas_call(
        body,
        grid=(2,),
        in_specs=first
        + [pl.BlockSpec((256, 512), lambda a: (a + 2 * half, 0)), column, column] + [once((512, 512))] * 2,
        out_specs=pl.BlockSpec((8, 32, 512), lambda a: (a + 2 * half, 0, 0)),
        out_shape=jax.ShapeDtypeStruct((32, 32, 512), f32),
        input_output_aliases=alias,
        compiler_params=pltpu.CompilerParams(vmem_limit_bytes=56 << 20),
        cost_estimate=pl.CostEstimate(flops=800000000, bytes_accessed=5 << 20, transcendentals=0),
        name="output",
    )(*given, x, ahi, alo, phi, plo)


def split(w):
    high = lax.reduce_precision(w, 8, 7)
    return high.astype(bf16), (w - high).astype(bf16)


def weights(gain, w_qkv, w_proj, rel_bias):
    root = 1.0 / math.sqrt(32.0)
    width = w_proj.shape[0]
    wc = gain[:, None] * w_qkv
    wc = wc * jnp.where(jnp.arange(3 * width) < width, root, 1.0)[None, :]
    wc = (wc - jnp.mean(wc, axis=0, keepdims=True)).T
    bias = rel_bias.reshape(4, 4, 64, 64).transpose(0, 3, 1, 2).reshape(4, 64, 256)
    return split(wc), split(w_proj), bias


ORDER = (0, 2, 1, 3)


def band_kernel(a_ref, b_ref, c_ref, d_ref, gain_ref, rows_ref, qkv_ref, proj_ref, gain_out, rel_ref):
    total = (a_ref[...] + b_ref[...]) + (c_ref[...] + d_ref[...])
    gain = gain_ref[...]
    sums = jnp.zeros((4, 128), f32)
    for k in range(12):
        part = total[4 * k : 4 * k + 4]
        cols = slice(128 * k, 128 * k + 128)
        qkv_ref[:, cols] = part * gain
        sums = sums + part * rows_ref[:, cols]
    for k in range(4):
        proj_ref[:, 128 * k : 128 * k + 128] = total[48 + 4 * k : 52 + 4 * k]
    rel_ref[...] = total[64:, :64]
    column = jnp.sum(sums, axis=1, keepdims=True)
    for n in range(4):
        gain_out[n] = column[n, 0]


def band_call(parts, gain, rows):
    return pl.pallas_call(
        band_kernel,
        out_shape=[
            jax.ShapeDtypeStruct((4, 1536), f32),
            jax.ShapeDtypeStruct((4, 512), f32),
            jax.ShapeDtypeStruct((4,), f32),
            jax.ShapeDtypeStruct((8, 64), f32),
        ],
        out_specs=[pl.BlockSpec(memory_space=pltpu.VMEM)] * 2
        + [pl.BlockSpec(memory_space=pltpu.SMEM), pl.BlockSpec(memory_space=pltpu.VMEM)],
        name="band",
    )(*parts, gain, rows)


def turn(size, by):
    return [(i, (i + by) % size) for i in range(size)]


def fetch(slots, plan_rank, plan_slot, early):
    count = lax.axis_size("buf")
    slot_count, tile_tokens, width = slots.shape[3:]
    part = tile_tokens // count
    spread = slots.reshape(slot_count, count, part, width).transpose(1, 0, 2, 3)
    held = lax.all_to_all(spread, "buf", split_axis=0, concat_axis=0, tiled=True)
    held, early = lax.optimization_barrier((held, early))
    held = held.reshape(count * slot_count, part, width)
    wanted = plan_rank.reshape(count) * slot_count + plan_slot.reshape(count)
    asked = held.at[wanted].get(mode="promise_in_bounds")
    tile = lax.all_to_all(asked, "buf", split_axis=0, concat_axis=0, tiled=True)
    return tile.reshape(32, 32, width), early


def edge_kernel(top_ref, side_ref, down_ref, right_ref, corner_ref):
    half = WSIDE // 2
    down_ref[...] = top_ref[...]
    right_ref[...] = side_ref[:, :half, :]
    corner_ref[...] = top_ref[:, :half, :]


def edge_call(tile):
    half, rows, width = WSIDE // 2, tile.shape[0], tile.shape[-1]
    return pl.pallas_call(
        edge_kernel,
        grid=(1,),
        in_specs=[
            pl.BlockSpec((half, rows, width), lambda a: (0, 0, 0)),
            pl.BlockSpec((rows, 16, width), lambda a: (0, 0, 0)),
        ],
        out_specs=[full((half, rows, width)), full((rows, half, width)), full((half, half, width))],
        out_shape=[
            jax.ShapeDtypeStruct(shape, bf16)
            for shape in ((half, rows, width), (rows, half, width), (half, half, width))
        ],
        compiler_params=pltpu.CompilerParams(vmem_limit_bytes=56 << 20),
        name="edges",
    )(tile, tile)


def halo(tile):
    lat, lon = lax.axis_size("lat"), lax.axis_size("lon")
    down, right, corner = edge_call(tile)
    down = lax.ppermute(down, "lat", turn(lat, -1))
    right = lax.ppermute(right, "lon", turn(lon, -1))
    corner_pairs = [
        (i * lon + j, (i - 1) % lat * lon + (j - 1) % lon) for i in range(lat) for j in range(lon)
    ]
    corner = lax.ppermute(corner, ("lat", "lon"), corner_pairs)
    return tile, down, right, corner


def send(blocks, axis, size, step):
    moved = [lax.ppermute(b, axis, turn(size, step * by)) for b, by in zip(blocks[1:], ORDER[1:])]
    return [blocks[0], *moved]


def choose(blocks, dim, me):
    return [lax.dynamic_index_in_dim(blocks, (me + by) % 4, dim, keepdims=False) for by in ORDER]


def total(parts):
    return (parts[0] + parts[1]) + (parts[2] + parts[3])


def sum_bands(own, other, work):
    buf, lat, lon = lax.axis_index("buf"), lax.axis_index("lat"), lax.axis_index("lon")
    got = lax.ppermute(other, "buf", [(i, i ^ 1) for i in range(8)])
    got, output = lax.optimization_barrier((got, work(0, None)))
    x = (own + got).reshape(9, 4, 4, 4, 8, 128)
    left = send(choose(x[:5], 3, lon), "lon", 4, 1)
    right = total(send(choose(x[5:], 2, lat), "lat", 4, 1))
    left, output = lax.optimization_barrier((left, work(1, output)))
    left = total(left)
    left = total(send(choose(left, 2, lat), "lat", 4, 1))
    right = total(send(choose(right, 2, lon), "lon", 4, 1))
    x = jnp.concatenate([left, right], axis=0)
    return output, [part.reshape(72, 128) for part in send(choose(x, 1, buf // 2), "buf", 8, 2)]


def on_device(slots, plan_rank, plan_slot, gain, w_qkv, w_proj, rel_bias, cotangent):
    width = gain.shape[0]
    wc, wp, bias = weights(gain, w_qkv, w_proj, rel_bias)
    tokens = 128 * cotangent.shape[1] * cotangent.shape[2] * cotangent.shape[3]
    ready = upstream_call(cotangent[0, 0], *wp, 1.0 / math.sqrt(tokens))
    place = (lax.axis_index("buf") * 4 + lax.axis_index("lat")) * 4 + lax.axis_index("lon")
    my_gain = jnp.broadcast_to(lax.dynamic_slice_in_dim(gain, place * 4, 4)[:, None], (4, 128))
    my_rows = lax.dynamic_slice_in_dim(w_qkv, place * 4, 4)
    last = lax.axis_index("lat") == lax.axis_size("lat") - 1
    flags = jnp.stack([last.astype(jnp.int32), lax.axis_index("buf") % 2])
    early = (ready, bias, wp, wc, my_gain, my_rows, flags)
    tile, early = fetch(slots, plan_rank, plan_slot, early)
    ready, bias, wp, wc, my_gain, my_rows, flags = early
    own, other, ahi, alo, x = main_call(flags, *halo(tile), *wc, bias, *ready)
    output, parts = sum_bands(own, other, lambda half, before: output_call(half, before, x, ahi, alo, *wp))
    grad_qkv, grad_proj, grad_gain, grad_rel = band_call(parts, my_gain, my_rows)
    return (output.reshape(cotangent.shape), grad_qkv, grad_proj, grad_gain, grad_rel)


def solution(mesh):
    placed = (
        P("buf", "lat", "lon", None, None, None),
        P("lat", "lon", None, None),
        P("lat", "lon", None),
        P(),
        P(),
        P(),
        P(),
        P("buf", None, "lat", "lon", None),
    )
    return jax.shard_map(
        on_device,
        mesh=mesh,
        in_specs=placed,
        out_specs=(
            P("buf", None, "lat", "lon", None),
            P(("buf", "lat", "lon"), None),
            P(("buf", "lat", "lon"), None),
            P(("buf", "lat", "lon")),
            P(("buf", "lat", "lon"), None),
        ),
        check_vma=False,
    )
```

```python
import functools
import math

import jax
import jax.numpy as jnp
from jax import lax
from jax.experimental import pallas as pl
from jax.experimental.pallas import tpu as pltpu
from jax.sharding import PartitionSpec as P

HEADS = 16
SPLIT = 5
WSIDE = 8
NT = (((1,), (1,)), ((), ()))
NN = (((1,), (0,)), ((), ()))
f32, bf16 = jnp.float32, jnp.bfloat16


def dot(left, right, dims=NN):
    return lax.dot_general(left, right, dims, preferred_element_type=f32)


def halves(value):
    high = value.astype(bf16)
    return high, (value - high.astype(f32)).astype(bf16)


def window_rows(block):
    pieces = [block[u, 8 * w : 8 * w + 8, :] for w in range(4) for u in range(8)]
    return jnp.concatenate(pieces, axis=0)


def upstream_kernel(scale, cot_ref, phi_ref, plo_ref, uhi_ref, ulo_ref, dohi_ref, dolo_ref, dotok_ref):
    upstream = window_rows(cot_ref) * scale
    uhi, ulo = halves(upstream)
    uhi_ref[...] = uhi
    ulo_ref[...] = ulo
    u3 = jnp.concatenate([uhi, uhi, ulo], axis=1)
    for at in range(0, 512, 128):
        phi = phi_ref[at : at + 128, :]
        rows = jnp.concatenate([phi, plo_ref[at : at + 128, :], phi], axis=1)
        hi, lo = halves(dot(rows, u3, NT))
        dohi_ref[at : at + 128, :], dolo_ref[at : at + 128, :] = hi, lo
        dotok_ref[:, 2 * at : 2 * at + 128] = hi.T
        dotok_ref[:, 2 * at + 128 : 2 * at + 256] = lo.T


def swap(value):
    return jnp.concatenate([value[:, 64:], value[:, :64]], axis=1)


def block_diagonal(value, left, right):
    other = swap(value)
    zeros = jnp.zeros((32, 128), bf16)
    for even, odd in ((value, other), (other, value)):
        first = jnp.concatenate([even[0:32] * left, odd[32:64] * right, zeros, zeros], axis=0)
        second = jnp.concatenate([zeros, zeros, even[64:96] * left, odd[96:128] * right], axis=0)
        yield jnp.concatenate([first, second], axis=1)


def gather_diagonal(lane, pair_a, pair_b):
    low = lane < 64
    return jnp.concatenate(
        [
            jnp.where(low, pair_a[:32], swap(pair_b[:32])),
            jnp.where(low, swap(pair_a[32:]), pair_b[32:]),
        ],
        axis=0,
    )


def heads_product(left2, hi, lo, window):
    zeros = jnp.zeros((64, 256), bf16)
    right = jnp.concatenate([hi, lo, hi, zeros] if window == 0 else [hi, lo, zeros, hi], axis=0)
    product = dot(left2, right)
    return [product[:64, :128], product[64:, 128:]]


def fill(source, step, slot, wcat, xt_all):
    pkhi, pklo, kt, vt, rstd_tok, rstd_lane, qt = slot
    here = pl.ds(pl.multiple_of(step * 256, 256), 256)
    kept = {}

    def project(first):
        for at in range(first, first + 512, 128):
            rows = slice(at, at + 128)
            pkhi[rows, :], pklo[rows, :] = halves(dot(wcat[rows, :], kept["twice"]) * kept["rstd"])

    def turned(base, tok):
        for g in range(4):
            rows = slice(base + 128 * g, base + 128 * g + 128)
            high = pkhi[rows, :].T
            tok[g, :, 0:128] = high
            tok[g, :, 128:256] = pklo[rows, :].T
            if base:
                tok[g, :, 256:384] = high

    def begin():
        tile, side, x_all = source
        rows = [tile[step * 8 + 4 + u].astype(f32) for u in range(8)]
        ends = [side[step * 8 + 4 + u].astype(f32) for u in range(8)]
        pieces = []
        for w in range(4):
            for u in range(8):
                if w < 3:
                    pieces.append(rows[u][8 * w + 4 : 8 * w + 12])
                else:
                    pieces.append(jnp.concatenate([rows[u][28:], ends[u]], axis=0))
        tokens16 = jnp.concatenate(pieces, axis=0).astype(bf16)
        x_all[here, :] = tokens16
        xt = tokens16.T.astype(f32)
        xt16 = xt.astype(bf16)
        xt_all[:, here] = xt16
        mean = jnp.sum(xt, axis=0, keepdims=True) * (1.0 / 512)
        centered = xt - mean
        spread = jnp.sum(centered * centered, axis=0, keepdims=True) * (1.0 / 512)
        rstd = lax.rsqrt(spread + 1e-05)
        rstd_lane[...] = rstd * jnp.ones((8, 1), f32)
        rstd_tok[...] = jnp.transpose(jnp.broadcast_to(rstd, (128, 256)))
        kept["rstd"] = rstd
        kept["twice"] = jnp.concatenate([xt16, xt16], axis=0)

    def queries():
        project(0)
        turned(0, qt)

    def keys():
        project(512)
        turned(512, kt)

    def values():
        project(1024)
        turned(1024, vt)

    return [begin, queries, keys, values]


def main_kernel(
    flag_ref, tile_hbm, down_hbm, right_hbm, corner_hbm, chi_hbm, clo_hbm, bias_hbm, uhi_hbm, ulo_hbm, dohi_ref, dolo_ref, dotok_ref,
    own_left, own_right, other_left, other_right, ahi_ref, alo_ref, x_hbm,
    pkhi0, pklo0, kt0, vt0, rt0, rl0, qt0, pkhi1, pklo1, kt1, vt1, rt1, rl1, qt1,
    xt_all, ahi_all, alo_all, g_all, rel_acc,
    wcat, bias_ref, uhi_ref, ulo_ref, own_ref, other_ref, tile, side, x_all, in_sem, out_sem,
):
    step = pl.program_id(0)
    slots = ((pkhi0, pklo0, kt0, vt0, rt0, rl0, qt0), (pkhi1, pklo1, kt1, vt1, rt1, rl1, qt1))
    loads = [
        pltpu.make_async_copy(source, target, in_sem.at[n])
        for n, (source, target) in enumerate(
            (
                (tile_hbm, tile.at[:32]),
                (down_hbm, tile.at[32:]),
                (right_hbm, side.at[:32]),
                (corner_hbm, side.at[32:]),
                (chi_hbm, wcat.at[:, :512]),
                (clo_hbm, wcat.at[:, 512:]),
                (bias_hbm, bias_ref),
                (uhi_hbm, uhi_ref),
                (ulo_hbm, ulo_ref),
            )
        )
    ]
    source = (tile, side, x_all)
    lane = lax.broadcasted_iota(jnp.int32, (1, 128), 1)
    left16 = (lane < 64).astype(f32).astype(bf16)
    right16 = (lane >= 64).astype(f32).astype(bf16)
    lane2 = lax.broadcasted_iota(jnp.int32, (1, 256), 1) & 127
    head_of = [((lane2 >= 32 * j) & (lane2 < 32 * j + 32)).astype(f32).astype(bf16) for j in range(4)]
    row_of = lax.broadcasted_iota(jnp.int32, (64, 256), 0)
    lane_of = lax.broadcasted_iota(jnp.int32, (64, 256), 1)
    root = 1.0 / math.sqrt(32.0)

    def operands(g, slot):
        pkhi, pklo, kt, vt = slot[:4]
        rows_q, rows_k, rows_v = (slice(128 * g + base, 128 * g + base + 128) for base in (0, 512, 1024))
        unit = []
        for p in range(2):
            lanes = slice(128 * p, 128 * p + 128)
            qhi = list(block_diagonal(pkhi[rows_q, lanes], left16, right16))
            qlo = list(block_diagonal(pklo[rows_q, lanes], left16, right16))
            ohi = list(block_diagonal(dohi_ref[rows_q, lanes], left16, right16))
            olo = list(block_diagonal(dolo_ref[rows_q, lanes], left16, right16))
            both = []
            for rows in (rows_k, rows_v):
                high, low = pkhi[rows, lanes], pklo[rows, lanes]
                other = swap(high)
                one = high * left16 + other * right16
                two = other * left16 + high * right16
                both.append([jnp.concatenate([one, low], axis=1), jnp.concatenate([two, low], axis=1)])
            for w in range(2):
                unit.append((qhi[w], qlo[w], ohi[w], olo[w], both[0][w], both[1][w]))
        scores, products = [], []
        for n, (qh, ql, oh, ol, _, _) in enumerate(unit):
            at = 64 * n
            scores.append(dot(kt[g, at : at + 64, :], jnp.concatenate([qh, qh, ql], axis=0)))
            products.append(dot(vt[g, at : at + 64, :], jnp.concatenate([oh, oh, ol], axis=0)))
        return unit, scores, products

    def finish(g, state, slot, edge):
        unit, scores, products = state
        rstd_tok, rstd_lane, qt = slot[4:]
        rows_q = slice(128 * g, 128 * g + 128)
        cols_k = slice(128 * g + 512, 128 * g + 640)
        cols_v = slice(128 * g + 1024, 128 * g + 1152)
        probs, attended, dss, grad_q = [], [], [], []
        for n in range(4):
            s = scores[n] + bias_ref[g]
            if edge is not None:
                s = jnp.where(edge, -1000000000.0, s)
            e = jnp.exp(s - jnp.max(s, axis=0, keepdims=True))
            weights = e * (1.0 / jnp.sum(e, axis=0, keepdims=True))
            inner = jnp.sum(weights * products[n], axis=0, keepdims=True)
            probs.append(halves(weights))
            dss.append(weights * (products[n] - inner))
        rel_acc[g] = rel_acc[g] + ((dss[0] + dss[1]) + (dss[2] + dss[3]))
        dss = [halves(ds) for ds in dss]
        for n in range(4):
            attended.append(heads_product(unit[n][5], *probs[n], n % 2))
        for n in range(4):
            grad_q.append(heads_product(unit[n][4], *dss[n], n % 2))
        for pairs, tok, cols in ((probs, None, cols_v), (dss, qt, cols_k)):
            for n in range(4):
                at = 64 * n
                if tok is None:
                    both = dotok_ref[at : at + 64, 256 * g : 256 * g + 256]
                else:
                    both = tok[g, at : at + 64, :]
                to = pl.ds(pl.multiple_of(step * 256 + at, 64), 64)
                to_lo = pl.ds(pl.multiple_of(step * 256 + at + 1024, 64), 64)
                product = dot(
                    jnp.concatenate(pairs[n], axis=0),
                    jnp.concatenate([both * mask for mask in head_of], axis=0),
                )
                total = product[:64, :128] + product[64:, :128] + product[:64, 128:]
                g_all[to, cols], g_all[to_lo, cols] = halves(total * rstd_tok[at : at + 64, :])
        for p in range(2):
            lanes = slice(128 * p, 128 * p + 128)
            here_p = pl.ds(pl.multiple_of(step * 256 + 128 * p, 128), 128)
            here_p_lo = pl.ds(pl.multiple_of(step * 256 + 128 * p + 1024, 128), 128)
            one, two = 2 * p, 2 * p + 1
            att = jnp.concatenate([gather_diagonal(lane, attended[one][t], attended[two][t]) for t in range(2)], axis=0)
            att_hi, att_lo = halves(att)
            ahi_all[rows_q, here_p], alo_all[rows_q, here_p] = att_hi, att_lo
            ahi_ref[rows_q, lanes], alo_ref[rows_q, lanes] = att_hi, att_lo
            gq = jnp.concatenate([gather_diagonal(lane, grad_q[one][t], grad_q[two][t]) for t in range(2)], axis=0)
            gq = gq * (rstd_lane[0:1, lanes] * root)
            gq_hi, gq_lo = halves(gq)
            g_all[here_p, rows_q], g_all[here_p_lo, rows_q] = gq_hi.T, gq_lo.T

    def attention(slot, beside, edge):
        state = operands(0, slot)
        for g in range(4):
            if beside is not None:
                beside[g]()
            after = operands(g + 1, slot) if g < 3 else None
            finish(g, state, slot, edge)
            state = after

    @pl.when(step == 0)
    def _():
        for load in loads:
            load.start()
        rel_acc[...] = jnp.zeros_like(rel_acc)
        parts = fill(source, 0, slots[0], wcat, xt_all)
        for load in loads[:4]:
            load.wait()
        parts[0]()
        loads[4].wait()
        loads[5].wait()
        for part in parts[1:]:
            part()
        loads[6].wait()

    @pl.when(step % 2 == 0)
    def _():
        attention(slots[0], fill(source, step + 1, slots[1], wcat, xt_all), None)

    @pl.when(step == 1)
    def _():
        attention(slots[1], fill(source, step + 1, slots[0], wcat, xt_all), None)

    @pl.when(step == 3)
    def _():
        keep = pltpu.make_async_copy(x_all, x_hbm, in_sem.at[9])
        keep.start()
        crossing = ((row_of >= 32) != ((lane_of & 63) >= 32)) & (flag_ref[0] > 0)
        attention(slots[1], None, crossing)
        loads[7].wait()
        loads[8].wait()
        sub = lax.broadcasted_iota(jnp.int32, (1, 8, 128), 1)
        first = flag_ref[1] == 0
        stores = [keep]

        def send(k):
            for n, (source, left, right) in enumerate(
                ((own_ref, own_left, own_right), (other_ref, other_left, other_right))
            ):
                target = left.at[k] if k < SPLIT else right.at[k - SPLIT]
                copy = pltpu.make_async_copy(source.at[k], target, out_sem.at[n, k])
                copy.start()
                stores.append(copy)

        def pack(k, value):
            a, b = value[:, :128].reshape(64, 8, 128), value[:, 128:].reshape(64, 8, 128)
            aa = jnp.concatenate([a[:, 4:], a[:, :4]], axis=1)
            bb = jnp.concatenate([b[:, 4:], b[:, :4]], axis=1)
            even = jnp.where(sub < 4, a, bb).reshape(4, 2, 8, 8, 128)
            odd = jnp.where(sub < 4, aa, b).reshape(4, 2, 8, 8, 128)
            for n, block in ((0, even), (1, odd)):
                own_ref[k, :, :, n] = jnp.where(first, block[:, 0], block[:, 1])
                other_ref[k, :, :, n] = jnp.where(first, block[:, 1], block[:, 0])
            send(k)

        twice = jnp.concatenate([xt_all[...], xt_all[...]], axis=1)
        for k in range(6):
            value = dot(twice, g_all[:, 256 * k : 256 * k + 256])
            pack(k, value - jnp.sum(value, axis=0, keepdims=True) * (1.0 / 512))
        for k in range(2):
            cols = slice(256 * k, 256 * k + 256)
            u = uhi_ref[:, cols]
            value = (
                dot(ahi_all[...], u) + dot(alo_all[...], u) + dot(ahi_all[...], ulo_ref[:, cols])
            )
            pack(6 + k, value)
        for g in range(4):
            turned = jnp.transpose(
                jnp.concatenate([rel_acc[g], jnp.zeros((64, 256), f32)], axis=0)
            ).reshape(2, 8, 2, 8, 128)
            own_ref[8, g] = jnp.where(first, turned[0], turned[1])
            other_ref[8, g] = jnp.where(first, turned[1], turned[0])
        send(8)
        for store in stores:
            store.wait()


def output_kernel(x_ref, ahi_ref, alo_ref, phi_ref, plo_ref, out_ref):
    tokens = x_ref[...].astype(f32)
    tok_hi, tok_lo = ahi_ref[...].T, alo_ref[...].T
    phi = phi_ref[...]
    wp3 = jnp.concatenate([phi, phi, plo_ref[...]], axis=0)
    result = tokens + dot(jnp.concatenate([tok_hi, tok_lo, tok_hi], axis=1), wp3)
    for w in range(4):
        for u in range(8):
            out_ref[u, 8 * w : 8 * w + 8, :] = result[64 * w + 8 * u : 64 * w + 8 * u + 8, :]


def full(shape):
    return pl.BlockSpec(shape, lambda a: (0,) * len(shape))


def once(shape):
    return pl.BlockSpec(shape, lambda a: (0,) * len(shape), pipeline_mode=pl.Buffered(1))


def upstream_call(cot, phi, plo, scale):
    return pl.pallas_call(
        functools.partial(upstream_kernel, scale),
        grid=(4,),
        in_specs=[pl.BlockSpec((8, 32, 512), lambda a: (a, 0, 0))] + [full((512, 512))] * 2,
        out_specs=[
            pl.BlockSpec((256, 512), lambda a: (a, 0)),
            pl.BlockSpec((256, 512), lambda a: (a, 0)),
            pl.BlockSpec((512, 256), lambda a: (0, a)),
            pl.BlockSpec((512, 256), lambda a: (0, a)),
            pl.BlockSpec((256, 1024), lambda a: (a, 0)),
        ],
        out_shape=[jax.ShapeDtypeStruct((1024, 512), bf16)] * 2
        + [jax.ShapeDtypeStruct((512, 1024), bf16)] * 2
        + [jax.ShapeDtypeStruct((1024, 1024), bf16)],
        compiler_params=pltpu.CompilerParams(vmem_limit_bytes=24 << 20),
        cost_estimate=pl.CostEstimate(flops=1600000000, bytes_accessed=8 << 20, transcendentals=0),
        name="upstream",
    )(cot, phi, plo)


def main_call(flags, tile, down, right, corner, chi, clo, bias, uhi, ulo, dohi, dolo, dotok):
    anywhere = pl.BlockSpec(memory_space=pl.ANY)
    column = pl.BlockSpec((512, 256), lambda a: (0, a))
    slot = [
        pltpu.VMEM((1536, 256), bf16),
        pltpu.VMEM((1536, 256), bf16),
        pltpu.VMEM((4, 256, 384), bf16),
        pltpu.VMEM((4, 256, 384), bf16),
        pltpu.VMEM((256, 128), f32),
        pltpu.VMEM((8, 256), f32),
        pltpu.VMEM((4, 256, 256), bf16),
    ]
    terms = (9, 4, 8, 2, 8, 128)
    return pl.pallas_call(
        main_kernel,
        grid=(4,),
        in_specs=[pl.BlockSpec(memory_space=pltpu.SMEM)]
        + [anywhere] * 9
        + [column] * 2
        + [pl.BlockSpec((256, 1024), lambda a: (a, 0))],
        out_specs=[anywhere] * 4 + [column] * 2 + [anywhere],
        out_shape=[jax.ShapeDtypeStruct((n, *terms[1:]), f32) for n in (SPLIT, 9 - SPLIT)] * 2
        + [jax.ShapeDtypeStruct((512, 1024), bf16)] * 2
        + [jax.ShapeDtypeStruct((1024, 512), bf16)],
        scratch_shapes=slot
        + slot
        + [
            pltpu.VMEM((512, 1024), bf16),
            pltpu.VMEM((512, 1024), bf16),
            pltpu.VMEM((512, 1024), bf16),
            pltpu.VMEM((2048, 1536), bf16),
            pltpu.VMEM((4, 64, 256), f32),
            pltpu.VMEM((1536, 1024), bf16),
            pltpu.VMEM((4, 64, 256), f32),
            pltpu.VMEM((1024, 512), bf16),
            pltpu.VMEM((1024, 512), bf16),
            pltpu.VMEM(terms, f32),
            pltpu.VMEM(terms, f32),
            pltpu.VMEM((36, 32, 512), bf16),
            pltpu.VMEM((36, 4, 512), bf16),
            pltpu.VMEM((1024, 512), bf16),
            pltpu.SemaphoreType.DMA((10,)),
            pltpu.SemaphoreType.DMA((2, 9)),
        ],
        compiler_params=pltpu.CompilerParams(vmem_limit_bytes=56 << 20),
        cost_estimate=pl.CostEstimate(flops=16000000000, bytes_accessed=24 << 20, transcendentals=1 << 20),
        name="block",
    )(flags, tile, down, right, corner, chi, clo, bias, uhi, ulo, dohi, dolo, dotok)


def output_call(half, before, x, ahi, alo, phi, plo):
    body, first, given, alias = output_kernel, [], [], {}
    if before is not None:
        first, given, alias = [pl.BlockSpec(memory_space=pl.ANY)], [before], {0: 0}

        def body(_, *refs):
            output_kernel(*refs)

    column = pl.BlockSpec((512, 256), lambda a: (0, a + 2 * half))
    return pl.pallas_call(
        body,
        grid=(2,),
        in_specs=first
        + [pl.BlockSpec((256, 512), lambda a: (a + 2 * half, 0)), column, column] + [once((512, 512))] * 2,
        out_specs=pl.BlockSpec((8, 32, 512), lambda a: (a + 2 * half, 0, 0)),
        out_shape=jax.ShapeDtypeStruct((32, 32, 512), f32),
        input_output_aliases=alias,
        compiler_params=pltpu.CompilerParams(vmem_limit_bytes=56 << 20),
        cost_estimate=pl.CostEstimate(flops=800000000, bytes_accessed=5 << 20, transcendentals=0),
        name="output",
    )(*given, x, ahi, alo, phi, plo)


def split(w):
    high = lax.reduce_precision(w, 8, 7)
    return high.astype(bf16), (w - high).astype(bf16)


def weights(gain, w_qkv, w_proj, rel_bias):
    root = 1.0 / math.sqrt(32.0)
    width = w_proj.shape[0]
    wc = gain[:, None] * w_qkv
    wc = wc * jnp.where(jnp.arange(3 * width) < width, root, 1.0)[None, :]
    wc = (wc - jnp.mean(wc, axis=0, keepdims=True)).T
    bias = rel_bias.reshape(4, 4, 64, 64).transpose(0, 3, 1, 2).reshape(4, 64, 256)
    return split(wc), split(w_proj), bias


ORDER = (0, 2, 1, 3)


def band_kernel(a_ref, b_ref, c_ref, d_ref, gain_ref, rows_ref, qkv_ref, proj_ref, gain_out, rel_ref):
    total = (a_ref[...] + b_ref[...]) + (c_ref[...] + d_ref[...])
    gain = gain_ref[...]
    sums = jnp.zeros((4, 128), f32)
    for k in range(12):
        part = total[4 * k : 4 * k + 4]
        cols = slice(128 * k, 128 * k + 128)
        qkv_ref[:, cols] = part * gain
        sums = sums + part * rows_ref[:, cols]
    for k in range(4):
        proj_ref[:, 128 * k : 128 * k + 128] = total[48 + 4 * k : 52 + 4 * k]
    rel_ref[...] = total[64:, :64]
    column = jnp.sum(sums, axis=1, keepdims=True)
    for n in range(4):
        gain_out[n] = column[n, 0]


def band_call(parts, gain, rows):
    return pl.pallas_call(
        band_kernel,
        out_shape=[
            jax.ShapeDtypeStruct((4, 1536), f32),
            jax.ShapeDtypeStruct((4, 512), f32),
            jax.ShapeDtypeStruct((4,), f32),
            jax.ShapeDtypeStruct((8, 64), f32),
        ],
        out_specs=[pl.BlockSpec(memory_space=pltpu.VMEM)] * 2
        + [pl.BlockSpec(memory_space=pltpu.SMEM), pl.BlockSpec(memory_space=pltpu.VMEM)],
        name="band",
    )(*parts, gain, rows)


def turn(size, by):
    return [(i, (i + by) % size) for i in range(size)]


def fetch(slots, plan_rank, plan_slot, early):
    count = lax.axis_size("buf")
    slot_count, tile_tokens, width = slots.shape[3:]
    part = tile_tokens // count
    spread = slots.reshape(slot_count, count, part, width).transpose(1, 0, 2, 3)
    held = lax.all_to_all(spread, "buf", split_axis=0, concat_axis=0, tiled=True)
    held, early = lax.optimization_barrier((held, early))
    held = held.reshape(count * slot_count, part, width)
    wanted = plan_rank.reshape(count) * slot_count + plan_slot.reshape(count)
    asked = held.at[wanted].get(mode="promise_in_bounds")
    tile = lax.all_to_all(asked, "buf", split_axis=0, concat_axis=0, tiled=True)
    return tile.reshape(32, 32, width), early


def edge_kernel(top_ref, side_ref, down_ref, right_ref, corner_ref):
    half = WSIDE // 2
    down_ref[...] = top_ref[...]
    right_ref[...] = side_ref[:, :half, :]
    corner_ref[...] = top_ref[:, :half, :]


def edge_call(tile):
    half, rows, width = WSIDE // 2, tile.shape[0], tile.shape[-1]
    return pl.pallas_call(
        edge_kernel,
        grid=(1,),
        in_specs=[
            pl.BlockSpec((half, rows, width), lambda a: (0, 0, 0)),
            pl.BlockSpec((rows, 16, width), lambda a: (0, 0, 0)),
        ],
        out_specs=[full((half, rows, width)), full((rows, half, width)), full((half, half, width))],
        out_shape=[
            jax.ShapeDtypeStruct(shape, bf16)
            for shape in ((half, rows, width), (rows, half, width), (half, half, width))
        ],
        compiler_params=pltpu.CompilerParams(vmem_limit_bytes=56 << 20),
        name="edges",
    )(tile, tile)


def halo(tile):
    lat, lon = lax.axis_size("lat"), lax.axis_size("lon")
    down, right, corner = edge_call(tile)
    down = lax.ppermute(down, "lat", turn(lat, -1))
    right = lax.ppermute(right, "lon", turn(lon, -1))
    corner_pairs = [
        (i * lon + j, (i - 1) % lat * lon + (j - 1) % lon) for i in range(lat) for j in range(lon)
    ]
    corner = lax.ppermute(corner, ("lat", "lon"), corner_pairs)
    return tile, down, right, corner


def send(blocks, axis, size, step):
    moved = [lax.ppermute(b, axis, turn(size, step * by)) for b, by in zip(blocks[1:], ORDER[1:])]
    return [blocks[0], *moved]


def choose(blocks, dim, me):
    return [lax.dynamic_index_in_dim(blocks, (me + by) % 4, dim, keepdims=False) for by in ORDER]


def total(parts):
    return (parts[0] + parts[1]) + (parts[2] + parts[3])


def sum_bands(terms, work):
    buf, lat, lon = lax.axis_index("buf"), lax.axis_index("lat"), lax.axis_index("lon")
    own_left, own_right, other_left, other_right = terms
    pairs = [(i, i ^ 1) for i in range(8)]
    got_left = lax.ppermute(other_left, "buf", pairs)
    got_right, output = lax.optimization_barrier((lax.ppermute(other_right, "buf", pairs), work(0, None)))
    left = (own_left + got_left).reshape(SPLIT, 4, 4, 4, 8, 128)
    right = (own_right + got_right).reshape(9 - SPLIT, 4, 4, 4, 8, 128)
    left = send(choose(left, 3, lon), "lon", 4, 1)
    right = total(send(choose(right, 2, lat), "lat", 4, 1))
    left, output = lax.optimization_barrier((left, work(1, output)))
    left = total(left)
    left = total(send(choose(left, 2, lat), "lat", 4, 1))
    right = total(send(choose(right, 2, lon), "lon", 4, 1))
    x = jnp.concatenate([left, right], axis=0)
    return output, [part.reshape(72, 128) for part in send(choose(x, 1, buf // 2), "buf", 8, 2)]


def on_device(slots, plan_rank, plan_slot, gain, w_qkv, w_proj, rel_bias, cotangent):
    width = gain.shape[0]
    wc, wp, bias = weights(gain, w_qkv, w_proj, rel_bias)
    tokens = 128 * cotangent.shape[1] * cotangent.shape[2] * cotangent.shape[3]
    ready = upstream_call(cotangent[0, 0], *wp, 1.0 / math.sqrt(tokens))
    place = (lax.axis_index("buf") * 4 + lax.axis_index("lat")) * 4 + lax.axis_index("lon")
    my_gain = jnp.broadcast_to(lax.dynamic_slice_in_dim(gain, place * 4, 4)[:, None], (4, 128))
    my_rows = lax.dynamic_slice_in_dim(w_qkv, place * 4, 4)
    last = lax.axis_index("lat") == lax.axis_size("lat") - 1
    flags = jnp.stack([last.astype(jnp.int32), lax.axis_index("buf") % 2])
    early = (ready, bias, wp, wc, my_gain, my_rows, flags)
    tile, early = fetch(slots, plan_rank, plan_slot, early)
    ready, bias, wp, wc, my_gain, my_rows, flags = early
    *terms, ahi, alo, x = main_call(flags, *halo(tile), *wc, bias, *ready)
    output, parts = sum_bands(terms, lambda half, before: output_call(half, before, x, ahi, alo, *wp))
    grad_qkv, grad_proj, grad_gain, grad_rel = band_call(parts, my_gain, my_rows)
    return (output.reshape(cotangent.shape), grad_qkv, grad_proj, grad_gain, grad_rel)


def solution(mesh):
    placed = (
        P("buf", "lat", "lon", None, None, None),
        P("lat", "lon", None, None),
        P("lat", "lon", None),
        P(),
        P(),
        P(),
        P(),
        P("buf", None, "lat", "lon", None),
    )
    return jax.shard_map(
        on_device,
        mesh=mesh,
        in_specs=placed,
        out_specs=(
            P("buf", None, "lat", "lon", None),
            P(("buf", "lat", "lon"), None),
            P(("buf", "lat", "lon"), None),
            P(("buf", "lat", "lon")),
            P(("buf", "lat", "lon"), None),
        ),
        check_vma=False,
    )
```
